32 devices in a mesh: gx: 4 (over y, core), gy: 8 (over z, x).
Axes of the slice: x: 2, y: 2, z: 4, core: 2. Of those that a mesh axis runs over, the one named last changes fastest.
Arguments:
- later_adjoint: bfloat16 [8, 32, 2, 192, 512], P('gx', 'gy'), may hold values from -6 to 6
- coupling: bfloat16 [8, 32, 2, 6, 192, 48], P('gx', 'gy'), may hold values from -0.375 to 0.375
- inverse_diag: bfloat16 [8, 32, 2, 192, 192], P('gx', 'gy'), may hold values from -0.2 to 1.2
- tile_mask: int32 [8, 32, 2, 6], P('gx', 'gy'), may hold values 0 or 1
- perf_cell: int32 [32, 64], P(('gx', 'gy')), may hold values from 0 to 1023
- perf_slot: int32 [32, 64], P(('gx', 'gy')), may hold values from 0 to 23
- perf_live: int32 [32, 64], P(('gx', 'gy')), may hold values from 0 to 1, as said below
- perf_coef: float32 [3, 32, 64], P(None, ('gx', 'gy')), may hold values from -1.2 to 1.2
- well_gain: float32 [768], P(('gx', 'gy')), may hold values from 0.3 to 1.5
- misfit: float32 [2, 768, 512], P(None, ('gx', 'gy')), may hold values from -6 to 6
Outputs:
- earlier_adjoint: bfloat16 [8, 32, 2, 192, 512], P('gx', 'gy')
- well_adjoint: bfloat16 [2, 768, 512], P(None, ('gx', 'gy'))
The draws below stay inside these ranges and needn't reach their ends.
Inputs may be any that keep to these rules, and one draw needn't show every extreme that they name: `perf_live`: some owner receives only used slots from every device.
All inputs are finite; a program needn't handle non-finite values. No bound on the sum of `tile_mask` on one device may be relied on, other than what follows from the above.
Results may differ from the reference program's by a relative error of at most 0.0015.
The reference program's roundings to bfloat16 on the way (of `adjoint`, `faces`, `message` and `source`) count: a program that leaves them out, or rounds other values in their place, can miss the bound.
Values may be sent and summed in bfloat16 or wider, within the bound.
A program may use at most 128 MiB of HBM per device.

```python
import math
import jax
import jax.numpy as jnp
from jax import lax

TILES_X = 2
TILES_Y = 4
TILES_Z = 2
ADJOINTS = 512
WELLS_DEV = 24
CAPACITY = 2
STEPS = 2
UNKNOWNS = 192
FACE_ROWS = 48
GRID_X = 8
GRID_Y = 32
CELLS_DEV = 1024
SLOTS = 64
WELLS = 768
N_GX = 4
N_GY = 8


def draw_inverse_diag(key, part):
    shape = (GRID_X, GRID_Y, TILES_Z, UNKNOWNS, UNKNOWNS)
    spread = 0.6 / UNKNOWNS ** 0.5
    noise = jax.random.truncated_normal(key, -4.0, 4.0, shape, jnp.float32) * spread
    row_ids = jnp.arange(UNKNOWNS, dtype=jnp.int32)[:, None]
    col_ids = jnp.arange(UNKNOWNS, dtype=jnp.int32)[None, :]
    identity = jnp.where(row_ids == col_ids, 1.0, 0.0).astype(jnp.float32)
    return (identity + noise).astype(jnp.bfloat16)


def draw_perf_live(key, part):
    owners = SLOTS // CAPACITY
    level_key = jax.random.fold_in(key, 11)
    hot_key = jax.random.fold_in(key, 12)
    slot_key = jax.random.fold_in(key, 13)
    levels = jax.random.randint(level_key, (owners,), 1, 5)
    hottest = jax.random.randint(hot_key, (), 0, owners)
    levels = jnp.where(jnp.arange(owners, dtype=jnp.int32) == hottest, 4, levels)
    owner_of_slot = jnp.arange(SLOTS, dtype=jnp.int32) // CAPACITY
    rolls = jax.random.randint(slot_key, (owners, SLOTS), 0, 4)
    return jnp.where(rolls < levels[owner_of_slot][None, :], 1, 0).astype(jnp.int32)


def place_ends(result, stream_key, low, high):
    longest = result.shape.index(max(result.shape))
    spots = []
    for shift in (0, 1):
        where = [jax.random.randint(jax.random.fold_in(stream_key, axis), (), 0, length) for axis, length in enumerate(result.shape)]
        where[longest] = (where[longest] + shift) % result.shape[longest]
        spots.append(tuple(where))
    return result.at[spots[0]].set(low).at[spots[1]].set(high)


def level_of(own_key, shape, cuts, smallest, largest):
    def one(axis_at, shards_of):
        heights = jax.random.uniform(jax.random.fold_in(jax.random.fold_in(own_key, 6), axis_at), (shards_of,), jnp.float32, smallest / len(cuts), largest / len(cuts))
        return jnp.repeat(jnp.exp(heights), shape[axis_at] // shards_of).reshape((-1,) + (1,) * (len(shape) - axis_at - 1))

    gain = one(*cuts[0])
    for cut in cuts[1:]:
        gain = gain * one(*cut)
    return gain


def normal_values(own_key, shape, scale, reach, cuts=(), kind=jnp.bfloat16):
    result = scale * jax.random.normal(own_key, shape, jnp.float32)
    if cuts:
        result = result * level_of(own_key, shape, cuts, -0.22, 0.18)
    return jnp.clip(result, -reach, reach).astype(kind)


def setup_inputs(seed: int = 0) -> dict:
    arg_keys = jax.random.split(jax.random.key(seed), 11)
    later_adjoint = normal_values(arg_keys[0], (GRID_X, GRID_Y, TILES_Z, UNKNOWNS, ADJOINTS), 1.0, 6.0, ((0, 4), (1, 8)))
    coupling = normal_values(arg_keys[1], (GRID_X, GRID_Y, TILES_Z, 6, UNKNOWNS, FACE_ROWS), (6 * FACE_ROWS) ** -0.5, 0.375, ((0, 4), (1, 8)))
    inverse_diag = draw_inverse_diag(jax.random.fold_in(arg_keys[10], 71), 0)
    tile_mask = place_ends((jax.random.randint(arg_keys[3], (GRID_X, GRID_Y, TILES_Z, 6), 0, 8) < 7).astype(jnp.int32), jax.random.fold_in(arg_keys[3], 1), 0, 1)
    perf_cell = place_ends(jax.random.randint(arg_keys[4], (N_GX * N_GY, SLOTS), 0, CELLS_DEV), jax.random.fold_in(arg_keys[4], 1), 0, CELLS_DEV - 1).astype(jnp.int32)
    perf_slot = place_ends(jax.random.randint(arg_keys[5], (N_GX * N_GY, SLOTS), 0, WELLS_DEV), jax.random.fold_in(arg_keys[5], 1), 0, WELLS_DEV - 1).astype(jnp.int32)
    perf_live = draw_perf_live(jax.random.fold_in(arg_keys[10], 71), 0)
    perf_coef = jnp.clip(jax.random.uniform(arg_keys[7], (3, N_GX * N_GY, SLOTS), jnp.float32, -1.2, 1.2) * level_of(arg_keys[7], (3, N_GX * N_GY, SLOTS), ((1, 32),), -0.4, 0.0), -1.2, 1.2)
    well_gain = jnp.clip(jnp.exp(math.log(1.5) - 1.60943787 * jax.random.uniform(arg_keys[8], (WELLS,), jnp.float32) ** level_of(arg_keys[8], (WELLS,), ((0, 32),), -0.2, 0.2)), 0.3, 1.5)
    misfit = normal_values(arg_keys[9], (STEPS, WELLS, ADJOINTS), 1.0, 6.0, ((1, 32),), jnp.float32)
    return {"later_adjoint": later_adjoint, "coupling": coupling, "inverse_diag": inverse_diag, "tile_mask": tile_mask, "perf_cell": perf_cell, "perf_slot": perf_slot, "perf_live": perf_live, "perf_coef": perf_coef, "well_gain": well_gain, "misfit": misfit}


def neighbour(values, axis, offset):
    extent = values.shape[axis]
    widths = [(0, 0)] * values.ndim
    widths[axis] = (1, 1)
    padded = jnp.pad(values, widths)
    return lax.slice_in_dim(padded, 1 + offset, 1 + offset + extent, axis=axis)


def face_stack(adjoint):
    columns = adjoint.shape[-1]
    cells = adjoint.reshape(GRID_X, GRID_Y, TILES_Z, 3, 4, 4, 4, columns)
    lower_x = neighbour(cells, 0, -1)[:, :, :, :, 3]
    upper_x = neighbour(cells, 0, 1)[:, :, :, :, 0]
    lower_y = neighbour(cells, 1, -1)[:, :, :, :, :, 3]
    upper_y = neighbour(cells, 1, 1)[:, :, :, :, :, 0]
    lower_z = neighbour(cells, 2, -1)[:, :, :, :, :, :, 3]
    upper_z = neighbour(cells, 2, 1)[:, :, :, :, :, :, 0]
    listed = [lower_x, upper_x, lower_y, upper_y, lower_z, upper_z]
    listed = [face.reshape(GRID_X, GRID_Y, TILES_Z, 48, columns) for face in listed]
    return jnp.stack(listed, axis=3)


def to_devices(values):
    columns = values.shape[-1]
    shaped = values.reshape(N_GX, TILES_X, N_GY, TILES_Y, TILES_Z, 192, columns)
    return shaped.transpose(0, 2, 1, 3, 4, 5, 6).reshape(N_GX * N_GY, TILES_X * TILES_Y * TILES_Z * 192, columns)


def from_devices(values):
    columns = values.shape[-1]
    shaped = values.reshape(N_GX, N_GY, TILES_X, TILES_Y, TILES_Z, 192, columns)
    return shaped.transpose(0, 2, 1, 3, 4, 5, 6).reshape(GRID_X, GRID_Y, TILES_Z, 192, columns)


def sweep(adjoint, misfit_step, coupling, inverse_diag, tile_mask, perf_cell, perf_slot, perf_live, perf_coef, well_gain):
    columns = adjoint.shape[-1]
    device_count = N_GX * N_GY
    faces = face_stack(adjoint) * tile_mask[..., None, None].astype(jnp.bfloat16)
    flux = jnp.einsum('abcdij,abcdjr->abcir', coupling.astype(jnp.float32), faces.astype(jnp.float32))
    adjoint_dev = to_devices(adjoint)
    flux_dev = to_devices(flux)
    tile_of = perf_cell // 64
    cell_of = perf_cell % 64
    in_use = perf_live.astype(jnp.float32)[:, :, None]
    message = jnp.zeros((device_count, SLOTS, columns), jnp.float32)
    row_list = []
    for component in range(3):
        row_index = (tile_of * 192 + component * 64 + cell_of).astype(jnp.int32)
        picked = jnp.take_along_axis(adjoint_dev, row_index[:, :, None], axis=1).astype(jnp.float32)
        message = message + perf_coef[component][:, :, None] * picked
        row_list.append(row_index)
    message = (in_use * message).astype(jnp.bfloat16)
    owner = (jnp.arange(SLOTS, dtype=jnp.int32) // CAPACITY)[None, :]
    well_id = (owner * WELLS_DEV + perf_slot).astype(jnp.int32).reshape(-1)
    summed = jax.ops.segment_sum(message.reshape(-1, columns).astype(jnp.float32), well_id, num_segments=WELLS)
    well_adj = (well_gain[:, None] * (summed + misfit_step)).astype(jnp.bfloat16)
    returned = well_adj[well_id].reshape(device_count, SLOTS, columns).astype(jnp.float32) * in_use
    device_ids = jnp.arange(device_count, dtype=jnp.int32)[:, None]
    for component in range(3):
        flux_dev = flux_dev.at[device_ids, row_list[component]].add(perf_coef[component][:, :, None] * returned)
    source = from_devices(flux_dev).astype(jnp.bfloat16)
    updated = -jnp.einsum('abcij,abcjr->abcir', inverse_diag.astype(jnp.float32), source.astype(jnp.float32))
    return updated.astype(jnp.bfloat16), well_adj


def reference(later_adjoint, coupling, inverse_diag, tile_mask, perf_cell, perf_slot, perf_live, perf_coef, well_gain, misfit):
    block_cols = min(ADJOINTS, 128)
    blocks = ADJOINTS // block_cols
    adjoint_blocks = later_adjoint.reshape(GRID_X, GRID_Y, TILES_Z, 192, blocks, block_cols).transpose(4, 0, 1, 2, 3, 5)
    misfit_blocks = misfit.reshape(STEPS, WELLS, blocks, block_cols).transpose(2, 0, 1, 3)

    def solve_block(block_pair):
        adjoint, misfit_block = block_pair
        collected = []
        for sweep_index in range(STEPS):
            adjoint, well_adj = sweep(adjoint, misfit_block[sweep_index], coupling, inverse_diag, tile_mask,
                                      perf_cell, perf_slot, perf_live, perf_coef, well_gain)
            collected.append(well_adj)
        return adjoint, jnp.stack(collected)

    adjoint_out, wells_out = lax.map(solve_block, (adjoint_blocks, misfit_blocks))
    earlier = adjoint_out.transpose(1, 2, 3, 4, 0, 5).reshape(GRID_X, GRID_Y, TILES_Z, 192, ADJOINTS)
    well_adjoint = wells_out.transpose(1, 2, 0, 3).reshape(STEPS, WELLS, ADJOINTS)
    return earlier, well_adjoint
```

```python
import functools
import jax
import jax.numpy as jnp
from jax import lax
from jax.experimental import pallas as pl
from jax.experimental.pallas import tpu as pltpu
from jax.sharding import PartitionSpec as P

CAPACITY = 2
STEPS = 2
MESH = pl.DeviceIdType.MESH
BF16 = jnp.bfloat16
F32 = jnp.float32
I32 = jnp.int32


def dot(a, b):
    return jnp.dot(a, b, preferred_element_type=F32)


def iota(shape, dim):
    return lax.broadcasted_iota(I32, shape, dim)


def kernel(
    n_gx,
    n_gy,
    adj_hbm,
    coup_hbm,
    inv_hbm,
    mask_ref,
    cell_ref,
    slot_ref,
    live_ref,
    coef_ref,
    gain_ref,
    misfit_hbm,
    out_hbm,
    wells_ref,
    adj0,
    adj1,
    outbuf,
    coup,
    inv,
    misfit,
    sel_face,
    gather_w,
    near_w,
    far_w,
    flux,
    face_ylo,
    face_yhi,
    face_z,
    halo_x,
    halo_y,
    message_acc,
    landed_rows,
    tag_out,
    tag_in,
    message_out,
    message_in,
    return_out,
    return_in,
    sel_rows,
    sel_wells,
    load_sems,
    out_sem,
    x_send,
    x_recv,
    y_send,
    y_recv,
    tag_send,
    tag_recv,
    message_send,
    message_recv,
    return_send,
    return_recv,
):
    n = n_gx * n_gy
    slots = CAPACITY * n
    tiles = adj0.shape[0]
    span_y = face_z.shape[2]
    columns = adj0.shape[-1]
    lanes = 128
    chunks = columns // lanes
    gx = lax.axis_index("gx")
    gy = lax.axis_index("gy")
    me = gx * n_gy + gy

    quarter = tiles // 4
    loads = [
        pltpu.make_async_copy(
            adj_hbm.at[pl.ds(q * quarter, quarter)],
            adj0.at[pl.ds(q * quarter, quarter)],
            load_sems.at[q],
        )
        for q in range(4)
    ]
    load_coup = pltpu.make_async_copy(coup_hbm, coup, load_sems.at[4])
    load_inv = pltpu.make_async_copy(inv_hbm, inv, load_sems.at[5])
    load_misfit = pltpu.make_async_copy(misfit_hbm, misfit.at[:, pl.ds(0, 24)], load_sems.at[6])
    for load in loads + [load_coup, load_inv, load_misfit]:
        load.start()

    barrier = pltpu.get_barrier_semaphore()

    def greet(d, carry):
        j = lax.rem(me + d, n)
        pl.semaphore_signal(
            barrier, inc=1, device_id=(j // n_gy, lax.rem(j, n_gy)), device_id_type=MESH
        )
        return carry

    lax.fori_loop(1, n, greet, 0)

    def fill_tag(p, carry):
        upper = iota((8, lanes), 0) < 4
        tag_out[p] = jnp.where(upper, slot_ref[0, 2 * p], slot_ref[0, 2 * p + 1])
        return carry

    lax.fori_loop(0, n, fill_tag, 0)

    row = iota((48, 192), 0)
    col = iota((48, 192), 1)
    start_y = (row // 4) * 16 + row % 4
    pick_ylo = jnp.where(col == start_y, 1.0, 0.0).astype(BF16)
    pick_yhi = jnp.where(col == start_y + 12, 1.0, 0.0).astype(BF16)
    for z in range(2):
        sel_face[z, 0:48] = pick_ylo
        sel_face[z, 48:96] = pick_yhi
        sel_face[z, 96:144] = jnp.where(col == 4 * row + 3 * (1 - z), 1.0, 0.0).astype(BF16)

    cell_row = jnp.concatenate([cell_ref[...], cell_ref[...]], axis=1)
    parts = []
    for k in range(3):
        coef = coef_ref[k] * live_ref[...].astype(F32)
        high = coef.astype(BF16).astype(F32)
        low = (coef - high).astype(BF16).astype(F32)
        parts.append(jnp.concatenate([high, low], axis=1))
    width = 2 * slots
    cell_col = jnp.broadcast_to(cell_row, (lanes, width)).T
    cell_col = jnp.concatenate([cell_col, cell_col[:, 0:64]], axis=1)
    lane = iota((width, 192), 1)
    wide = [jnp.broadcast_to(part, (lanes, width)).T for part in parts]
    wide = [jnp.concatenate([w, w[:, 0:64]], axis=1) for w in wide]
    coef_cols = jnp.where(lane < 64, wide[0], jnp.where(lane < 128, wide[1], wide[2]))
    shifted_col = cell_col - lane % 64
    coef_rows = jnp.concatenate(
        [jnp.broadcast_to(part, (64, width)) for part in parts], axis=0
    )
    shifted_row = jnp.broadcast_to(cell_row, (192, width)) - iota((192, width), 0) % 64

    def place(t, carry):
        gather_w[t] = jnp.where(shifted_col == 64 * t, coef_cols, 0.0).astype(BF16)
        far_w[t, :, 0:width] = jnp.where(shifted_row == 64 * t, coef_rows, 0.0).astype(BF16)
        return carry

    lax.fori_loop(0, tiles, place, 0)
    misfit[:, 24:32] = jnp.zeros((STEPS, 8, columns), F32)

    half = tiles // 2

    @pl.when(gx == 0)
    def _():
        halo_x[:, 0:half] = jnp.zeros((STEPS, half) + halo_x.shape[2:], BF16)

    @pl.when(gx == n_gx - 1)
    def _():
        halo_x[:, half:tiles] = jnp.zeros((STEPS, half) + halo_x.shape[2:], BF16)

    @pl.when(gy == 0)
    def _():
        halo_y[:, 0] = jnp.zeros((STEPS,) + halo_y.shape[2:], BF16)

    @pl.when(gy == n_gy - 1)
    def _():
        halo_y[:, 1] = jnp.zeros((STEPS,) + halo_y.shape[2:], BF16)

    pl.semaphore_wait(barrier, n - 1)

    def spread(source, target, send, recv):
        own = pltpu.make_async_copy(source.at[me], target.at[me], recv)
        own.start()

        def one(d, carry):
            j = lax.rem(me + d, n)
            pltpu.make_async_remote_copy(
                src_ref=source.at[j],
                dst_ref=target.at[me],
                send_sem=send,
                recv_sem=recv,
                device_id=(j // n_gy, lax.rem(j, n_gy)),
                device_id_type=MESH,
            ).start()
            return carry

        lax.fori_loop(1, n, one, 0)

    def wait_all(target, recv):
        pltpu.make_async_copy(target, target, recv).wait()

    def wait_sent(source, send):
        part = source.at[pl.ds(0, n - 1)]
        pltpu.make_async_copy(part, part, send).wait()

    spread(tag_out, tag_in, tag_send, tag_recv)

    def x_copies(src, s):
        up = pltpu.make_async_remote_copy(
            src_ref=src.at[pl.ds(half, half), :, 3],
            dst_ref=halo_x.at[s, pl.ds(0, half)],
            send_sem=x_send.at[s, 0],
            recv_sem=x_recv.at[s, 0],
            device_id=(gx + 1, gy),
            device_id_type=MESH,
        )
        down = pltpu.make_async_remote_copy(
            src_ref=src.at[pl.ds(0, half), :, 0],
            dst_ref=halo_x.at[s, pl.ds(half, half)],
            send_sem=x_send.at[s, 1],
            recv_sem=x_recv.at[s, 1],
            device_id=(gx - 1, gy),
            device_id_type=MESH,
        )
        return up, down

    def y_copies(s):
        up = pltpu.make_async_remote_copy(
            src_ref=face_yhi.at[s, :, span_y - 1],
            dst_ref=halo_y.at[s, 0],
            send_sem=y_send.at[s, 0],
            recv_sem=y_recv.at[s, 0],
            device_id=(gx, gy + 1),
            device_id_type=MESH,
        )
        down = pltpu.make_async_remote_copy(
            src_ref=face_ylo.at[s, :, 0],
            dst_ref=halo_y.at[s, 1],
            send_sem=y_send.at[s, 1],
            recv_sem=y_recv.at[s, 1],
            device_id=(gx, gy - 1),
            device_id_type=MESH,
        )
        return up, down

    def for_pairs(y, body):
        def one(i, carry):
            x = i // 2
            z = i % 2
            body(x, z, (x * span_y + y) * 2 + z)
            return carry

        lax.fori_loop(0, 4, one, 0)

    for load in loads:
        load.wait()

    for s in range(STEPS):
        src = adj0 if s == 0 else adj1
        dst = adj1 if s == 0 else outbuf
        x_up, x_down = x_copies(src, s)
        y_up, y_down = y_copies(s)

        @pl.when(gx < n_gx - 1)
        def _():
            x_up.start()

        @pl.when(gx > 0)
        def _():
            x_down.start()

        message_acc[...] = jnp.zeros_like(message_acc)

        def faces(y):
            def body(x, z, t):
                whole = src[t].reshape(192, columns)
                left = jnp.concatenate([sel_face[z], gather_w[t]], axis=0)
                got = dot(left, whole)
                face_ylo[s, x, y, z] = got[0:48].astype(BF16)
                face_yhi[s, x, y, z] = got[48:96].astype(BF16)
                face_z[s, x, y, z] = got[96:144].astype(BF16)
                message_acc[...] += got[144:]

            for_pairs(y, body)

        faces(0)

        @pl.when(gy > 0)
        def _():
            y_down.start()

        faces(span_y - 1)

        @pl.when(gy < n_gy - 1)
        def _():
            y_up.start()

        for y in range(1, span_y - 1):
            faces(y)

        message = message_acc[0:slots] + message_acc[slots:width]
        message = message.astype(BF16).astype(F32)
        for q in range(chunks):
            flat = message_out.at[s].reshape(n * 8, lanes)
            flat[pl.ds(q, slots, stride=chunks), :] = message[:, q * lanes : (q + 1) * lanes]
        spread(message_out.at[s], message_in.at[s], message_send.at[s], message_recv.at[s])

        if s == 0:
            load_coup.wait()

            def weights(y):
                def body(x, z, t):
                    def block(d):
                        keep = mask_ref[x, y, z, d] != 0
                        return jnp.where(keep, coup[t, d], jnp.zeros((192, 48), BF16))

                    near = [block(1 - x), block(5 - z)]
                    far = [block(x)]
                    (near if y > 0 else far).append(block(2))
                    (near if y < span_y - 1 else far).append(block(3))
                    near_w[t, :, 0 : 48 * len(near)] = jnp.concatenate(near, axis=1)
                    far_w[t, :, width : width + 48 * len(far)] = jnp.concatenate(far, axis=1)

                for_pairs(y, body)

            for y in range(span_y):
                weights(y)

        def near_flux(y):
            def body(x, z, t):
                beside = ((1 - x) * span_y + y) * 2 + z
                listed = [src[beside, :, 3 * x].reshape(48, columns), face_z[s, x, y, 1 - z]]
                if y > 0:
                    listed.append(face_yhi[s, x, y - 1, z])
                if y < span_y - 1:
                    listed.append(face_ylo[s, x, y + 1, z])
                flux[t] = dot(near_w[t, :, 0 : 48 * len(listed)], jnp.concatenate(listed, axis=0))

            for_pairs(y, body)

        for y in range(span_y):
            near_flux(y)

        if s == 0:
            load_misfit.wait()
            wait_all(tag_in, tag_recv)
            tags = tag_in.reshape(n * 8, lanes)[pl.ds(0, slots, stride=4), :]
            chosen = jnp.where(tags == iota((slots, lanes), 1), 1.0, 0.0)
            sel_rows[...] = chosen.astype(BF16)
            sel_wells[...] = chosen.T[0:32].astype(BF16)
        wait_all(message_in.at[s], message_recv.at[s])
        flat_in = message_in.at[s].reshape(n * 8, lanes)
        arrived = jnp.concatenate(
            [flat_in[pl.ds(q, slots, stride=chunks), :] for q in range(chunks)], axis=1
        ).astype(BF16)
        gain_row = iota((32, 1), 0)
        gain = jnp.zeros((32, 1), F32)
        for w in range(24):
            gain = jnp.where(gain_row == w, gain_ref[w], gain)
        well = (gain * (dot(sel_wells[...], arrived) + misfit[s])).astype(BF16)
        wells_ref[s] = well.astype(F32)[0:24]
        returned = dot(sel_rows[:, 0:32], well)
        flat_out = return_out.at[s].reshape(n * 8, lanes)
        for q in range(chunks):
            flat_out[pl.ds(q, slots, stride=chunks), :] = returned[:, q * lanes : (q + 1) * lanes]
        spread(return_out.at[s], return_in.at[s], return_send.at[s], return_recv.at[s])

        @pl.when(gx > 0)
        def _():
            x_up.wait_recv()

        @pl.when(gx < n_gx - 1)
        def _():
            x_down.wait_recv()

        @pl.when(gy > 0)
        def _():
            y_up.wait_recv()

        @pl.when(gy < n_gy - 1)
        def _():
            y_down.wait_recv()

        if s == 0:
            load_inv.wait()
        wait_all(return_in.at[s], return_recv.at[s])
        flat_back = return_in.at[s].reshape(n * 8, lanes)
        landed = jnp.concatenate(
            [flat_back[pl.ds(q, slots, stride=chunks), :] for q in range(chunks)], axis=1
        ).astype(BF16)
        landed_rows[0:slots] = landed
        landed_rows[slots:width] = landed

        def finish(y):
            def body(x, z, t):
                listed = [landed_rows[...], halo_x[s, t].reshape(48, columns)]
                if y == 0:
                    listed.append(halo_y[s, 0, x, z])
                if y == span_y - 1:
                    listed.append(halo_y[s, 1, x, z])
                depth = width + 48 * (len(listed) - 1)
                added = dot(far_w[t, :, 0:depth], jnp.concatenate(listed, axis=0))
                source = (flux[t] + added).astype(BF16)
                new = (-dot(inv[t], source)).astype(BF16)
                dst[t] = new.reshape(3, 4, 16, columns)
                if s == STEPS - 1:
                    pltpu.make_async_copy(dst.at[t], out_hbm.at[t], out_sem).start()

            for_pairs(y, body)

        for y in range(span_y):
            finish(y)

    for s in range(STEPS):
        x_up, x_down = x_copies(adj0 if s == 0 else adj1, s)
        y_up, y_down = y_copies(s)

        @pl.when(gx < n_gx - 1)
        def _():
            x_up.wait_send()

        @pl.when(gx > 0)
        def _():
            x_down.wait_send()

        @pl.when(gy < n_gy - 1)
        def _():
            y_up.wait_send()

        @pl.when(gy > 0)
        def _():
            y_down.wait_send()

        wait_sent(message_out.at[s], message_send.at[s])
        wait_sent(return_out.at[s], return_send.at[s])
    wait_sent(tag_out, tag_send)
    pltpu.make_async_copy(outbuf, out_hbm, out_sem).wait()


def local(
    n_gx,
    n_gy,
    later_adjoint,
    coupling,
    inverse_diag,
    tile_mask,
    perf_cell,
    perf_slot,
    perf_live,
    perf_coef,
    well_gain,
    misfit,
):
    span_x, span_y, span_z, unknowns, columns = later_adjoint.shape
    tiles = span_x * span_y * span_z
    n = n_gx * n_gy
    slots = CAPACITY * n
    width = 2 * slots
    adj = later_adjoint.reshape(tiles, 3, 4, 16, columns)
    coup = coupling.reshape(tiles, 6, 192, 48)
    inv = inverse_diag.reshape(tiles, 192, 192)
    any_space = pl.BlockSpec(memory_space=pl.ANY)
    vmem = pl.BlockSpec(memory_space=pltpu.VMEM)
    smem = pl.BlockSpec(memory_space=pltpu.SMEM)
    dma = pltpu.SemaphoreType.DMA
    block = (n, 8, 128)
    face = (STEPS, span_x, span_y, span_z, 48, columns)
    out, wells = pl.pallas_call(
        functools.partial(kernel, n_gx, n_gy),
        out_shape=(
            jax.ShapeDtypeStruct(adj.shape, BF16),
            jax.ShapeDtypeStruct((STEPS, 24, columns), F32),
        ),
        in_specs=[any_space] * 3 + [smem, vmem, smem, vmem, vmem, smem, any_space],
        out_specs=(any_space, vmem),
        scratch_shapes=[
            pltpu.VMEM(adj.shape, BF16),
            pltpu.VMEM(adj.shape, BF16),
            pltpu.VMEM(adj.shape, BF16),
            pltpu.VMEM(coup.shape, BF16),
            pltpu.VMEM(inv.shape, BF16),
            pltpu.VMEM((STEPS, 32, columns), F32),
            pltpu.VMEM((2, 144, 192), BF16),
            pltpu.VMEM((tiles, width, 192), BF16),
            pltpu.VMEM((tiles, 192, 192), BF16),
            pltpu.VMEM((tiles, 192, width + 96), BF16),
            pltpu.VMEM((tiles, 192, columns), F32),
            pltpu.VMEM(face, BF16),
            pltpu.VMEM(face, BF16),
            pltpu.VMEM(face, BF16),
            pltpu.VMEM((STEPS, tiles, 3, 16, columns), BF16),
            pltpu.VMEM((STEPS, 2, span_x, span_z, 48, columns), BF16),
            pltpu.VMEM((width, columns), F32),
            pltpu.VMEM((width, columns), BF16),
            pltpu.VMEM(block, I32),
            pltpu.VMEM(block, I32),
            pltpu.VMEM((STEPS,) + block, F32),
            pltpu.VMEM((STEPS,) + block, F32),
            pltpu.VMEM((STEPS,) + block, F32),
            pltpu.VMEM((STEPS,) + block, F32),
            pltpu.VMEM((slots, 128), BF16),
            pltpu.VMEM((32, slots), BF16),
            dma((7,)),
            dma,
            dma((STEPS, 2)),
            dma((STEPS, 2)),
            dma((STEPS, 2)),
            dma((STEPS, 2)),
            dma,
            dma,
            dma((STEPS,)),
            dma((STEPS,)),
            dma((STEPS,)),
            dma((STEPS,)),
        ],
        compiler_params=pltpu.CompilerParams(
            collective_id=0, has_side_effects=True, vmem_limit_bytes=56 * 1024 * 1024
        ),
    )(
        adj,
        coup,
        inv,
        tile_mask,
        perf_cell,
        perf_slot,
        perf_live,
        perf_coef,
        well_gain,
        misfit,
    )
    return out.reshape(later_adjoint.shape), wells.astype(BF16)


def solution(mesh):
    return jax.shard_map(
        functools.partial(local, mesh.shape["gx"], mesh.shape["gy"]),
        mesh=mesh,
        in_specs=(
            P("gx", "gy", None, None, None),
            P("gx", "gy", None, None, None, None),
            P("gx", "gy", None, None, None),
            P("gx", "gy", None, None),
            P(("gx", "gy"), None),
            P(("gx", "gy"), None),
            P(("gx", "gy"), None),
            P(None, ("gx", "gy"), None),
            P(("gx", "gy")),
            P(None, ("gx", "gy"), None),
        ),
        out_specs=(P("gx", "gy", None, None, None), P(None, ("gx", "gy"), None)),
        check_vma=False,
    )
```

```python
import functools
import jax
import jax.numpy as jnp
from jax import lax
from jax.experimental import pallas as pl
from jax.experimental.pallas import tpu as pltpu
from jax.sharding import PartitionSpec as P

CAPACITY = 2
STEPS = 2
MESH = pl.DeviceIdType.MESH
BF16 = jnp.bfloat16
F32 = jnp.float32
I32 = jnp.int32


def dot(a, b):
    return jnp.dot(a, b, preferred_element_type=F32)


def iota(shape, dim):
    return lax.broadcasted_iota(I32, shape, dim)


def kernel(
    n_gx,
    n_gy,
    adj_hbm,
    coup_hbm,
    inv_hbm,
    mask_ref,
    cell_ref,
    slot_ref,
    live_ref,
    coef_ref,
    gain_ref,
    misfit_hbm,
    source_hbm,
    wells_ref,
    adj0,
    adj1,
    outbuf,
    coup,
    inv,
    misfit,
    sel_face,
    gather_w,
    near_w,
    far_w,
    flux,
    face_ylo,
    face_yhi,
    face_z,
    halo_x,
    halo_y,
    message_acc,
    landed_rows,
    tag_out,
    tag_in,
    message_out,
    message_in,
    return_out,
    return_in,
    sel_rows,
    sel_wells,
    load_sems,
    out_sem,
    x_send,
    x_recv,
    y_send,
    y_recv,
    tag_send,
    tag_recv,
    message_send,
    message_recv,
    return_send,
    return_recv,
):
    n = n_gx * n_gy
    slots = CAPACITY * n
    tiles = adj0.shape[0]
    span_y = face_z.shape[2]
    columns = adj0.shape[-1]
    lanes = 128
    chunks = columns // lanes
    gx = lax.axis_index("gx")
    gy = lax.axis_index("gy")
    me = gx * n_gy + gy

    quarter = tiles // 4
    loads = [
        pltpu.make_async_copy(
            adj_hbm.at[pl.ds(q * quarter, quarter)],
            adj0.at[pl.ds(q * quarter, quarter)],
            load_sems.at[q],
        )
        for q in range(4)
    ]
    load_coup = pltpu.make_async_copy(coup_hbm, coup, load_sems.at[4])
    load_inv = pltpu.make_async_copy(inv_hbm, inv, load_sems.at[5])
    load_misfit = pltpu.make_async_copy(misfit_hbm, misfit.at[:, pl.ds(0, 24)], load_sems.at[6])
    for load in loads + [load_coup, load_inv, load_misfit]:
        load.start()

    barrier = pltpu.get_barrier_semaphore()

    def greet(d, carry):
        j = lax.rem(me + d, n)
        pl.semaphore_signal(
            barrier, inc=1, device_id=(j // n_gy, lax.rem(j, n_gy)), device_id_type=MESH
        )
        return carry

    lax.fori_loop(1, n, greet, 0)

    def fill_tag(p, carry):
        upper = iota((8, lanes), 0) < 4
        tag_out[p] = jnp.where(upper, slot_ref[0, 2 * p], slot_ref[0, 2 * p + 1])
        return carry

    lax.fori_loop(0, n, fill_tag, 0)

    row = iota((48, 192), 0)
    col = iota((48, 192), 1)
    start_y = (row // 4) * 16 + row % 4
    pick_ylo = jnp.where(col == start_y, 1.0, 0.0).astype(BF16)
    pick_yhi = jnp.where(col == start_y + 12, 1.0, 0.0).astype(BF16)
    for z in range(2):
        sel_face[z, 0:48] = pick_ylo
        sel_face[z, 48:96] = pick_yhi
        sel_face[z, 96:144] = jnp.where(col == 4 * row + 3 * (1 - z), 1.0, 0.0).astype(BF16)

    cell_row = jnp.concatenate([cell_ref[...], cell_ref[...]], axis=1)
    parts = []
    for k in range(3):
        coef = coef_ref[k] * live_ref[...].astype(F32)
        high = coef.astype(BF16).astype(F32)
        low = (coef - high).astype(BF16).astype(F32)
        parts.append(jnp.concatenate([high, low], axis=1))
    width = 2 * slots
    cell_col = jnp.broadcast_to(cell_row, (lanes, width)).T
    cell_col = jnp.concatenate([cell_col, cell_col[:, 0:64]], axis=1)
    lane = iota((width, 192), 1)
    wide = [jnp.broadcast_to(part, (lanes, width)).T for part in parts]
    wide = [jnp.concatenate([w, w[:, 0:64]], axis=1) for w in wide]
    coef_cols = jnp.where(lane < 64, wide[0], jnp.where(lane < 128, wide[1], wide[2]))
    shifted_col = cell_col - lane % 64
    coef_rows = jnp.concatenate(
        [jnp.broadcast_to(part, (64, width)) for part in parts], axis=0
    )
    shifted_row = jnp.broadcast_to(cell_row, (192, width)) - iota((192, width), 0) % 64

    def place(t, carry):
        gather_w[t] = jnp.where(shifted_col == 64 * t, coef_cols, 0.0).astype(BF16)
        far_w[t, :, 0:width] = jnp.where(shifted_row == 64 * t, coef_rows, 0.0).astype(BF16)
        return carry

    lax.fori_loop(0, tiles, place, 0)
    misfit[:, 24:32] = jnp.zeros((STEPS, 8, columns), F32)

    half = tiles // 2

    @pl.when(gx == 0)
    def _():
        halo_x[:, 0:half] = jnp.zeros((STEPS, half) + halo_x.shape[2:], BF16)

    @pl.when(gx == n_gx - 1)
    def _():
        halo_x[:, half:tiles] = jnp.zeros((STEPS, half) + halo_x.shape[2:], BF16)

    @pl.when(gy == 0)
    def _():
        halo_y[:, 0] = jnp.zeros((STEPS,) + halo_y.shape[2:], BF16)

    @pl.when(gy == n_gy - 1)
    def _():
        halo_y[:, 1] = jnp.zeros((STEPS,) + halo_y.shape[2:], BF16)

    pl.semaphore_wait(barrier, n - 1)

    def spread(source, target, send, recv):
        own = pltpu.make_async_copy(source.at[me], target.at[me], recv)
        own.start()

        def one(d, carry):
            j = lax.rem(me + d, n)
            pltpu.make_async_remote_copy(
                src_ref=source.at[j],
                dst_ref=target.at[me],
                send_sem=send,
                recv_sem=recv,
                device_id=(j // n_gy, lax.rem(j, n_gy)),
                device_id_type=MESH,
            ).start()
            return carry

        lax.fori_loop(1, n, one, 0)

    def wait_all(target, recv):
        pltpu.make_async_copy(target, target, recv).wait()

    def wait_sent(source, send):
        part = source.at[pl.ds(0, n - 1)]
        pltpu.make_async_copy(part, part, send).wait()

    spread(tag_out, tag_in, tag_send, tag_recv)

    def x_copies(src, s):
        up = pltpu.make_async_remote_copy(
            src_ref=src.at[pl.ds(half, half), :, 3],
            dst_ref=halo_x.at[s, pl.ds(0, half)],
            send_sem=x_send.at[s, 0],
            recv_sem=x_recv.at[s, 0],
            device_id=(gx + 1, gy),
            device_id_type=MESH,
        )
        down = pltpu.make_async_remote_copy(
            src_ref=src.at[pl.ds(0, half), :, 0],
            dst_ref=halo_x.at[s, pl.ds(half, half)],
            send_sem=x_send.at[s, 1],
            recv_sem=x_recv.at[s, 1],
            device_id=(gx - 1, gy),
            device_id_type=MESH,
        )
        return up, down

    def y_copies(s):
        up = pltpu.make_async_remote_copy(
            src_ref=face_yhi.at[s, :, span_y - 1],
            dst_ref=halo_y.at[s, 0],
            send_sem=y_send.at[s, 0],
            recv_sem=y_recv.at[s, 0],
            device_id=(gx, gy + 1),
            device_id_type=MESH,
        )
        down = pltpu.make_async_remote_copy(
            src_ref=face_ylo.at[s, :, 0],
            dst_ref=halo_y.at[s, 1],
            send_sem=y_send.at[s, 1],
            recv_sem=y_recv.at[s, 1],
            device_id=(gx, gy - 1),
            device_id_type=MESH,
        )
        return up, down

    def for_pairs(y, body):
        for x in range(2):
            for z in range(2):
                body(x, z, (x * span_y + y) * 2 + z)

    y_order = [0, span_y - 1] + list(range(1, span_y - 1))

    def start_x(src, s):
        x_up, x_down = x_copies(src, s)

        @pl.when(gx < n_gx - 1)
        def _():
            x_up.start()

        @pl.when(gx > 0)
        def _():
            x_down.start()

    def faces(src, s, y):
        y_up, y_down = y_copies(s)

        def body(x, z, t):
            whole = src[t].reshape(192, columns)
            left = jnp.concatenate([sel_face[z], gather_w[t]], axis=0)
            got = dot(left, whole)
            face_ylo[s, x, y, z] = got[0:48].astype(BF16)
            face_yhi[s, x, y, z] = got[48:96].astype(BF16)
            face_z[s, x, y, z] = got[96:144].astype(BF16)
            if y == 0 and x == 0 and z == 0:
                message_acc[...] = got[144:]
            else:
                message_acc[...] += got[144:]

        for_pairs(y, body)
        if y == 0:

            @pl.when(gy > 0)
            def _():
                y_down.start()

        if y == span_y - 1:

            @pl.when(gy < n_gy - 1)
            def _():
                y_up.start()

    for load in loads:
        load.wait()
    start_x(adj0, 0)
    for y in y_order:
        faces(adj0, 0, y)

    for s in range(STEPS):
        src = adj0 if s == 0 else adj1
        x_up, x_down = x_copies(src, s)
        y_up, y_down = y_copies(s)

        message = message_acc[0:slots] + message_acc[slots:width]
        message = message.astype(BF16).astype(F32)
        for q in range(chunks):
            flat = message_out.at[s].reshape(n * 8, lanes)
            flat[pl.ds(q, slots, stride=chunks), :] = message[:, q * lanes : (q + 1) * lanes]
        spread(message_out.at[s], message_in.at[s], message_send.at[s], message_recv.at[s])

        if s == 0:
            load_coup.wait()

            def weights(y):
                def body(x, z, t):
                    def block(d):
                        keep = mask_ref[x, y, z, d] != 0
                        return jnp.where(keep, coup[t, d], jnp.zeros((48, 192), BF16))

                    near = [block(1 - x), block(5 - z)]
                    far = [block(x)]
                    (near if y > 0 else far).append(block(2))
                    (near if y < span_y - 1 else far).append(block(3))
                    near_w[t, :, 0 : 48 * len(near)] = jnp.concatenate(near, axis=0).T
                    far_w[t, :, width : width + 48 * len(far)] = jnp.concatenate(far, axis=0).T

                for_pairs(y, body)

            for y in range(span_y):
                weights(y)

        def near_flux(y):
            def body(x, z, t):
                beside = ((1 - x) * span_y + y) * 2 + z
                listed = [src[beside, :, 3 * x].reshape(48, columns), face_z[s, x, y, 1 - z]]
                if y > 0:
                    listed.append(face_yhi[s, x, y - 1, z])
                if y < span_y - 1:
                    listed.append(face_ylo[s, x, y + 1, z])
                flux[t] = dot(near_w[t, :, 0 : 48 * len(listed)], jnp.concatenate(listed, axis=0))

            for_pairs(y, body)

        for y in range(span_y):
            near_flux(y)

        if s == 0:
            load_misfit.wait()
            wait_all(tag_in, tag_recv)
            tags = tag_in.reshape(n * 8, lanes)[pl.ds(0, slots, stride=4), :]
            chosen = jnp.where(tags == iota((slots, lanes), 1), 1.0, 0.0)
            sel_rows[...] = chosen.astype(BF16)
            sel_wells[...] = chosen.T[0:32].astype(BF16)
        wait_all(message_in.at[s], message_recv.at[s])
        flat_in = message_in.at[s].reshape(n * 8, lanes)
        arrived = jnp.concatenate(
            [flat_in[pl.ds(q, slots, stride=chunks), :] for q in range(chunks)], axis=1
        ).astype(BF16)
        gain_row = iota((32, 1), 0)
        gain = jnp.zeros((32, 1), F32)
        for w in range(24):
            gain = jnp.where(gain_row == w, gain_ref[w], gain)
        well = (gain * (dot(sel_wells[...], arrived) + misfit[s])).astype(BF16)
        wells_ref[s] = well.astype(F32)[0:24]
        returned = dot(sel_rows[:, 0:32], well)
        flat_out = return_out.at[s].reshape(n * 8, lanes)
        for q in range(chunks):
            flat_out[pl.ds(q, slots, stride=chunks), :] = returned[:, q * lanes : (q + 1) * lanes]
        spread(return_out.at[s], return_in.at[s], return_send.at[s], return_recv.at[s])

        @pl.when(gx > 0)
        def _():
            x_up.wait_recv()

        @pl.when(gx < n_gx - 1)
        def _():
            x_down.wait_recv()

        @pl.when(gy > 0)
        def _():
            y_up.wait_recv()

        @pl.when(gy < n_gy - 1)
        def _():
            y_down.wait_recv()

        if s == 0:
            load_inv.wait()
        wait_all(return_in.at[s], return_recv.at[s])
        flat_back = return_in.at[s].reshape(n * 8, lanes)
        landed = jnp.concatenate(
            [flat_back[pl.ds(q, slots, stride=chunks), :] for q in range(chunks)], axis=1
        ).astype(BF16)
        landed_rows[0:slots] = landed
        landed_rows[slots:width] = landed

        def far_source(x, y, z):
            t = (x * span_y + y) * 2 + z
            listed = [landed_rows[...], halo_x[s, t].reshape(48, columns)]
            if y == 0:
                listed.append(halo_y[s, 0, x, z])
            if y == span_y - 1:
                listed.append(halo_y[s, 1, x, z])
            depth = width + 48 * (len(listed) - 1)
            added = dot(far_w[t, :, 0:depth], jnp.concatenate(listed, axis=0))
            return (flux[t] + added).astype(BF16)

        for y in y_order:
            pairs = [(x, z) for x in range(2) for z in range(2)]
            ready = far_source(0, y, 0)
            for i, (x, z) in enumerate(pairs):
                t = (x * span_y + y) * 2 + z
                source = ready
                if i + 1 < len(pairs):
                    ready = far_source(pairs[i + 1][0], y, pairs[i + 1][1])
                if s < STEPS - 1:
                    new = (-dot(inv[t], source)).astype(BF16)
                    adj1[t] = new.reshape(3, 4, 16, columns)
                else:
                    outbuf[t] = source
            if s < STEPS - 1:
                if y == y_order[-1]:
                    start_x(adj1, s + 1)
                faces(adj1, s + 1, y)
            else:
                for x in range(2):
                    rows = pl.ds((x * span_y + y) * 2, 2)
                    pltpu.make_async_copy(outbuf.at[rows], source_hbm.at[rows], out_sem).start()

    for s in range(STEPS):
        x_up, x_down = x_copies(adj0 if s == 0 else adj1, s)
        y_up, y_down = y_copies(s)

        @pl.when(gx < n_gx - 1)
        def _():
            x_up.wait_send()

        @pl.when(gx > 0)
        def _():
            x_down.wait_send()

        @pl.when(gy < n_gy - 1)
        def _():
            y_up.wait_send()

        @pl.when(gy > 0)
        def _():
            y_down.wait_send()

        wait_sent(message_out.at[s], message_send.at[s])
        wait_sent(return_out.at[s], return_send.at[s])
    wait_sent(tag_out, tag_send)
    pltpu.make_async_copy(outbuf, source_hbm, out_sem).wait()


def last_product(source_ref, inv_ref, wells_ref, out_ref, rounded_ref):
    for i in range(source_ref.shape[0]):
        out_ref[i] = (-dot(inv_ref[i], source_ref[i])).astype(BF16)

    @pl.when(pl.program_id(0) == 0)
    def _():
        rounded_ref[...] = wells_ref[...].astype(BF16)


def local(
    n_gx,
    n_gy,
    later_adjoint,
    coupling,
    inverse_diag,
    tile_mask,
    perf_cell,
    perf_slot,
    perf_live,
    perf_coef,
    well_gain,
    misfit,
):
    span_x, span_y, span_z, unknowns, columns = later_adjoint.shape
    tiles = span_x * span_y * span_z
    n = n_gx * n_gy
    slots = CAPACITY * n
    width = 2 * slots
    adj = later_adjoint.reshape(tiles, 3, 4, 16, columns)
    coup = jnp.swapaxes(coupling.reshape(tiles, 6, 192, 48), 2, 3)
    inv = inverse_diag.reshape(tiles, 192, 192)
    any_space = pl.BlockSpec(memory_space=pl.ANY)
    vmem = pl.BlockSpec(memory_space=pltpu.VMEM)
    smem = pl.BlockSpec(memory_space=pltpu.SMEM)
    dma = pltpu.SemaphoreType.DMA
    block = (n, 8, 128)
    face = (STEPS, span_x, span_y, span_z, 48, columns)
    source, wells = pl.pallas_call(
        functools.partial(kernel, n_gx, n_gy),
        out_shape=(
            jax.ShapeDtypeStruct((tiles, 192, columns), BF16),
            jax.ShapeDtypeStruct((STEPS, 24, columns), F32),
        ),
        in_specs=[any_space] * 3 + [smem, vmem, smem, vmem, vmem, smem, any_space],
        out_specs=(any_space, vmem),
        scratch_shapes=[
            pltpu.VMEM(adj.shape, BF16),
            pltpu.VMEM(adj.shape, BF16),
            pltpu.VMEM((tiles, 192, columns), BF16),
            pltpu.VMEM(coup.shape, BF16),
            pltpu.VMEM(inv.shape, BF16),
            pltpu.VMEM((STEPS, 32, columns), F32),
            pltpu.VMEM((2, 144, 192), BF16),
            pltpu.VMEM((tiles, width, 192), BF16),
            pltpu.VMEM((tiles, 192, 192), BF16),
            pltpu.VMEM((tiles, 192, width + 96), BF16),
            pltpu.VMEM((tiles, 192, columns), F32),
            pltpu.VMEM(face, BF16),
            pltpu.VMEM(face, BF16),
            pltpu.VMEM(face, BF16),
            pltpu.VMEM((STEPS, tiles, 3, 16, columns), BF16),
            pltpu.VMEM((STEPS, 2, span_x, span_z, 48, columns), BF16),
            pltpu.VMEM((width, columns), F32),
            pltpu.VMEM((width, columns), BF16),
            pltpu.VMEM(block, I32),
            pltpu.VMEM(block, I32),
            pltpu.VMEM((STEPS,) + block, F32),
            pltpu.VMEM((STEPS,) + block, F32),
            pltpu.VMEM((STEPS,) + block, F32),
            pltpu.VMEM((STEPS,) + block, F32),
            pltpu.VMEM((slots, 128), BF16),
            pltpu.VMEM((32, slots), BF16),
            dma((7,)),
            dma,
            dma((STEPS, 2)),
            dma((STEPS, 2)),
            dma((STEPS, 2)),
            dma((STEPS, 2)),
            dma,
            dma,
            dma((STEPS,)),
            dma((STEPS,)),
            dma((STEPS,)),
            dma((STEPS,)),
        ],
        compiler_params=pltpu.CompilerParams(
            collective_id=0, has_side_effects=True, vmem_limit_bytes=56 * 1024 * 1024
        ),
    )(
        adj,
        coup,
        inv,
        tile_mask,
        perf_cell,
        perf_slot,
        perf_live,
        perf_coef,
        well_gain,
        misfit,
    )
    pair = 2
    out, rounded = pl.pallas_call(
        last_product,
        grid=(tiles // pair,),
        out_shape=(
            jax.ShapeDtypeStruct((tiles, 192, columns), BF16),
            jax.ShapeDtypeStruct(wells.shape, BF16),
        ),
        in_specs=[
            pl.BlockSpec((pair, 192, columns), lambda i: (i, 0, 0)),
            pl.BlockSpec((pair, 192, 192), lambda i: (i, 0, 0)),
            pl.BlockSpec(wells.shape, lambda i: (0, 0, 0)),
        ],
        out_specs=(
            pl.BlockSpec((pair, 192, columns), lambda i: (i, 0, 0)),
            pl.BlockSpec(wells.shape, lambda i: (0, 0, 0)),
        ),
        compiler_params=pltpu.CompilerParams(vmem_limit_bytes=16 * 1024 * 1024),
    )(source, inv, wells)
    return out.reshape(later_adjoint.shape), rounded


def solution(mesh):
    return jax.shard_map(
        functools.partial(local, mesh.shape["gx"], mesh.shape["gy"]),
        mesh=mesh,
        in_specs=(
            P("gx", "gy", None, None, None),
            P("gx", "gy", None, None, None, None),
            P("gx", "gy", None, None, None),
            P("gx", "gy", None, None),
            P(("gx", "gy"), None),
            P(("gx", "gy"), None),
            P(("gx", "gy"), None),
            P(None, ("gx", "gy"), None),
            P(("gx", "gy")),
            P(None, ("gx", "gy"), None),
        ),
        out_specs=(P("gx", "gy", None, None, None), P(None, ("gx", "gy"), None)),
        check_vma=False,
    )
```

```python
import functools
import jax
import jax.numpy as jnp
from jax import lax
from jax.experimental import pallas as pl
from jax.experimental.pallas import tpu as pltpu
from jax.sharding import PartitionSpec as P

CAPACITY = 2
STEPS = 2
MESH = pl.DeviceIdType.MESH
BF16 = jnp.bfloat16
F32 = jnp.float32
I32 = jnp.int32


def dot(a, b):
    return jnp.dot(a, b, preferred_element_type=F32)


def iota(shape, dim):
    return lax.broadcasted_iota(I32, shape, dim)


def kernel(
    n_gx,
    n_gy,
    adj_hbm,
    coup_hbm,
    inv_hbm,
    mask_ref,
    cell_ref,
    slot_ref,
    live_ref,
    coef_ref,
    gain_ref,
    misfit_hbm,
    source_hbm,
    wells_ref,
    adj0,
    adj1,
    outbuf,
    coup,
    inv,
    misfit,
    sel_face,
    gather_w,
    near_w,
    far_w,
    flux,
    face_ylo,
    face_yhi,
    face_z,
    halo_x,
    halo_y,
    message_acc,
    landed_rows,
    tag_out,
    tag_in,
    message_out,
    message_in,
    return_out,
    return_in,
    sel_rows,
    sel_wells,
    load_sems,
    out_sem,
    x_send,
    x_recv,
    y_send,
    y_recv,
    tag_send,
    tag_recv,
    message_send,
    message_recv,
    return_send,
    return_recv,
):
    n = n_gx * n_gy
    slots = CAPACITY * n
    tiles = adj0.shape[0]
    span_y = face_z.shape[2]
    columns = adj0.shape[-1]
    lanes = 128
    chunks = columns // lanes
    piece = 256
    cuts = [slice(c, c + piece) for c in range(0, columns, piece)]
    gx = lax.axis_index("gx")
    gy = lax.axis_index("gy")
    me = gx * n_gy + gy

    quarter = tiles // 4
    loads = [
        pltpu.make_async_copy(
            adj_hbm.at[pl.ds(q * quarter, quarter)],
            adj0.at[pl.ds(q * quarter, quarter)],
            load_sems.at[q],
        )
        for q in range(4)
    ]
    load_coup = pltpu.make_async_copy(coup_hbm, coup, load_sems.at[4])
    load_inv = pltpu.make_async_copy(inv_hbm, inv, load_sems.at[5])
    load_misfit = pltpu.make_async_copy(misfit_hbm, misfit.at[:, pl.ds(0, 24)], load_sems.at[6])
    for load in loads + [load_coup, load_inv, load_misfit]:
        load.start()

    barrier = pltpu.get_barrier_semaphore()

    def greet(d, carry):
        j = lax.rem(me + d, n)
        pl.semaphore_signal(
            barrier, inc=1, device_id=(j // n_gy, lax.rem(j, n_gy)), device_id_type=MESH
        )
        return carry

    lax.fori_loop(1, n, greet, 0)

    def fill_tag(p, carry):
        upper = iota((8, lanes), 0) < 4
        tag_out[p] = jnp.where(upper, slot_ref[0, 2 * p], slot_ref[0, 2 * p + 1])
        return carry

    lax.fori_loop(0, n, fill_tag, 0)

    row = iota((48, 192), 0)
    col = iota((48, 192), 1)
    start_y = (row // 4) * 16 + row % 4
    pick_ylo = jnp.where(col == start_y, 1.0, 0.0).astype(BF16)
    pick_yhi = jnp.where(col == start_y + 12, 1.0, 0.0).astype(BF16)
    for z in range(2):
        sel_face[z, 0:48] = pick_ylo
        sel_face[z, 48:96] = pick_yhi
        sel_face[z, 96:144] = jnp.where(col == 4 * row + 3 * (1 - z), 1.0, 0.0).astype(BF16)

    cell_row = jnp.concatenate([cell_ref[...], cell_ref[...]], axis=1)
    parts = []
    for k in range(3):
        coef = coef_ref[k] * live_ref[...].astype(F32)
        high = coef.astype(BF16).astype(F32)
        low = (coef - high).astype(BF16).astype(F32)
        parts.append(jnp.concatenate([high, low], axis=1))
    width = 2 * slots
    cell_col = jnp.broadcast_to(cell_row, (lanes, width)).T
    cell_col = jnp.concatenate([cell_col, cell_col[:, 0:64]], axis=1)
    lane = iota((width, 192), 1)
    wide = [jnp.broadcast_to(part, (lanes, width)).T for part in parts]
    wide = [jnp.concatenate([w, w[:, 0:64]], axis=1) for w in wide]
    coef_cols = jnp.where(lane < 64, wide[0], jnp.where(lane < 128, wide[1], wide[2]))
    shifted_col = cell_col - lane % 64
    coef_rows = jnp.concatenate(
        [jnp.broadcast_to(part, (64, width)) for part in parts], axis=0
    )
    shifted_row = jnp.broadcast_to(cell_row, (192, width)) - iota((192, width), 0) % 64

    def place(t, carry):
        gather_w[t] = jnp.where(shifted_col == 64 * t, coef_cols, 0.0).astype(BF16)
        far_w[t, :, 0:width] = jnp.where(shifted_row == 64 * t, coef_rows, 0.0).astype(BF16)
        return carry

    lax.fori_loop(0, tiles, place, 0)
    misfit[:, 24:32] = jnp.zeros((STEPS, 8, columns), F32)

    half = tiles // 2

    @pl.when(gx == 0)
    def _():
        halo_x[:, 0:half] = jnp.zeros((STEPS, half) + halo_x.shape[2:], BF16)

    @pl.when(gx == n_gx - 1)
    def _():
        halo_x[:, half:tiles] = jnp.zeros((STEPS, half) + halo_x.shape[2:], BF16)

    @pl.when(gy == 0)
    def _():
        halo_y[:, 0] = jnp.zeros((STEPS,) + halo_y.shape[2:], BF16)

    @pl.when(gy == n_gy - 1)
    def _():
        halo_y[:, 1] = jnp.zeros((STEPS,) + halo_y.shape[2:], BF16)

    pl.semaphore_wait(barrier, n - 1)

    def spread(source, target, send, recv):
        own = pltpu.make_async_copy(source.at[me], target.at[me], recv)
        own.start()

        def one(d, carry):
            j = lax.rem(me + d, n)
            pltpu.make_async_remote_copy(
                src_ref=source.at[j],
                dst_ref=target.at[me],
                send_sem=send,
                recv_sem=recv,
                device_id=(j // n_gy, lax.rem(j, n_gy)),
                device_id_type=MESH,
            ).start()
            return carry

        lax.fori_loop(1, n, one, 0)

    def wait_all(target, recv):
        pltpu.make_async_copy(target, target, recv).wait()

    def wait_sent(source, send):
        part = source.at[pl.ds(0, n - 1)]
        pltpu.make_async_copy(part, part, send).wait()

    spread(tag_out, tag_in, tag_send, tag_recv)

    def x_copies(src, s):
        up = pltpu.make_async_remote_copy(
            src_ref=src.at[pl.ds(half, half), :, 3],
            dst_ref=halo_x.at[s, pl.ds(0, half)],
            send_sem=x_send.at[s, 0],
            recv_sem=x_recv.at[s, 0],
            device_id=(gx + 1, gy),
            device_id_type=MESH,
        )
        down = pltpu.make_async_remote_copy(
            src_ref=src.at[pl.ds(0, half), :, 0],
            dst_ref=halo_x.at[s, pl.ds(half, half)],
            send_sem=x_send.at[s, 1],
            recv_sem=x_recv.at[s, 1],
            device_id=(gx - 1, gy),
            device_id_type=MESH,
        )
        return up, down

    def y_copies(s):
        up = pltpu.make_async_remote_copy(
            src_ref=face_yhi.at[s, :, span_y - 1],
            dst_ref=halo_y.at[s, 0],
            send_sem=y_send.at[s, 0],
            recv_sem=y_recv.at[s, 0],
            device_id=(gx, gy + 1),
            device_id_type=MESH,
        )
        down = pltpu.make_async_remote_copy(
            src_ref=face_ylo.at[s, :, 0],
            dst_ref=halo_y.at[s, 1],
            send_sem=y_send.at[s, 1],
            recv_sem=y_recv.at[s, 1],
            device_id=(gx, gy - 1),
            device_id_type=MESH,
        )
        return up, down

    def for_pairs(y, body):
        for x in range(2):
            for z in range(2):
                body(x, z, (x * span_y + y) * 2 + z)

    y_order = [0, span_y - 1] + list(range(1, span_y - 1))

    def start_x(src, s):
        x_up, x_down = x_copies(src, s)

        @pl.when(gx < n_gx - 1)
        def _():
            x_up.start()

        @pl.when(gx > 0)
        def _():
            x_down.start()

    def faces(src, s, y):
        y_up, y_down = y_copies(s)

        def body(x, z, t):
            for cut in cuts:
                whole = src[t, :, :, :, cut].reshape(192, piece)
                got = dot(sel_face[z], whole)
                face_ylo[s, x, y, z, :, cut] = got[0:48].astype(BF16)
                face_yhi[s, x, y, z, :, cut] = got[48:96].astype(BF16)
                face_z[s, x, y, z, :, cut] = got[96:144].astype(BF16)
                term = dot(gather_w[t], whole)
                if y == 0 and x == 0 and z == 0:
                    message_acc[:, cut] = term
                else:
                    message_acc[:, cut] += term

        for_pairs(y, body)
        if y == 0:

            @pl.when(gy > 0)
            def _():
                y_down.start()

        if y == span_y - 1:

            @pl.when(gy < n_gy - 1)
            def _():
                y_up.start()

    for load in loads:
        load.wait()
    start_x(adj0, 0)
    for y in y_order:
        faces(adj0, 0, y)

    for s in range(STEPS):
        src = adj0 if s == 0 else adj1
        x_up, x_down = x_copies(src, s)
        y_up, y_down = y_copies(s)

        message = message_acc[0:slots] + message_acc[slots:width]
        message = message.astype(BF16).astype(F32)
        for q in range(chunks):
            flat = message_out.at[s].reshape(n * 8, lanes)
            flat[pl.ds(q, slots, stride=chunks), :] = message[:, q * lanes : (q + 1) * lanes]
        spread(message_out.at[s], message_in.at[s], message_send.at[s], message_recv.at[s])

        if s == 0:
            load_coup.wait()

            def weights(y):
                def body(x, z, t):
                    def block(d):
                        keep = mask_ref[x, y, z, d] != 0
                        return jnp.where(keep, coup[t, d], jnp.zeros((48, 192), BF16))

                    near = [block(1 - x), block(5 - z)]
                    far = [block(x)]
                    (near if y > 0 else far).append(block(2))
                    (near if y < span_y - 1 else far).append(block(3))
                    near_w[t, :, 0 : 48 * len(near)] = jnp.concatenate(near, axis=0).T
                    far_w[t, :, width : width + 48 * len(far)] = jnp.concatenate(far, axis=0).T

                for_pairs(y, body)

            for y in range(span_y):
                weights(y)

        def near_flux(y):
            def body(x, z, t):
                beside = ((1 - x) * span_y + y) * 2 + z
                for cut in cuts:
                    listed = [src[beside, :, 3 * x, :, cut].reshape(48, piece)]
                    listed.append(face_z[s, x, y, 1 - z, :, cut])
                    if y > 0:
                        listed.append(face_yhi[s, x, y - 1, z, :, cut])
                    if y < span_y - 1:
                        listed.append(face_ylo[s, x, y + 1, z, :, cut])
                    depth = 48 * len(listed)
                    flux[t, :, cut] = dot(near_w[t, :, 0:depth], jnp.concatenate(listed, axis=0))

            for_pairs(y, body)

        for y in range(span_y):
            near_flux(y)

        if s == 0:
            load_misfit.wait()
            wait_all(tag_in, tag_recv)
            tags = tag_in.reshape(n * 8, lanes)[pl.ds(0, slots, stride=4), :]
            chosen = jnp.where(tags == iota((slots, lanes), 1), 1.0, 0.0)
            sel_rows[...] = chosen.astype(BF16)
            sel_wells[...] = chosen.T[0:32].astype(BF16)
        wait_all(message_in.at[s], message_recv.at[s])
        flat_in = message_in.at[s].reshape(n * 8, lanes)
        arrived = jnp.concatenate(
            [flat_in[pl.ds(q, slots, stride=chunks), :] for q in range(chunks)], axis=1
        ).astype(BF16)
        gain_row = iota((32, 1), 0)
        gain = jnp.zeros((32, 1), F32)
        for w in range(24):
            gain = jnp.where(gain_row == w, gain_ref[w], gain)
        well = (gain * (dot(sel_wells[...], arrived) + misfit[s])).astype(BF16)
        wells_ref[s] = well.astype(F32)[0:24]
        returned = dot(sel_rows[:, 0:32], well)
        flat_out = return_out.at[s].reshape(n * 8, lanes)
        for q in range(chunks):
            flat_out[pl.ds(q, slots, stride=chunks), :] = returned[:, q * lanes : (q + 1) * lanes]
        spread(return_out.at[s], return_in.at[s], return_send.at[s], return_recv.at[s])

        @pl.when(gx > 0)
        def _():
            x_up.wait_recv()

        @pl.when(gx < n_gx - 1)
        def _():
            x_down.wait_recv()

        @pl.when(gy > 0)
        def _():
            y_up.wait_recv()

        @pl.when(gy < n_gy - 1)
        def _():
            y_down.wait_recv()

        if s == 0:
            load_inv.wait()
        wait_all(return_in.at[s], return_recv.at[s])
        flat_back = return_in.at[s].reshape(n * 8, lanes)
        landed = jnp.concatenate(
            [flat_back[pl.ds(q, slots, stride=chunks), :] for q in range(chunks)], axis=1
        ).astype(BF16)
        landed_rows[0:slots] = landed
        landed_rows[slots:width] = landed

        def far_source(y, x, z, cut):
            t = (x * span_y + y) * 2 + z
            listed = [landed_rows[:, cut], halo_x[s, t, :, :, cut].reshape(48, piece)]
            if y == 0:
                listed.append(halo_y[s, 0, x, z, :, cut])
            if y == span_y - 1:
                listed.append(halo_y[s, 1, x, z, :, cut])
            depth = width + 48 * (len(listed) - 1)
            added = dot(far_w[t, :, 0:depth], jnp.concatenate(listed, axis=0))
            return (flux[t, :, cut] + added).astype(BF16)

        for y in y_order:
            items = [(x, z, cut) for x in range(2) for z in range(2) for cut in cuts]
            ready = far_source(y, *items[0])
            for i, (x, z, cut) in enumerate(items):
                t = (x * span_y + y) * 2 + z
                source = ready
                if i + 1 < len(items):
                    ready = far_source(y, *items[i + 1])
                if s < STEPS - 1:
                    new = (-dot(inv[t], source)).astype(BF16)
                    adj1[t, :, :, :, cut] = new.reshape(3, 4, 16, piece)
                else:
                    outbuf[t, :, cut] = source
            if s < STEPS - 1:
                if y == y_order[-1]:
                    start_x(adj1, s + 1)
                faces(adj1, s + 1, y)
            else:
                for x in range(2):
                    rows = pl.ds((x * span_y + y) * 2, 2)
                    pltpu.make_async_copy(outbuf.at[rows], source_hbm.at[rows], out_sem).start()

    for s in range(STEPS):
        x_up, x_down = x_copies(adj0 if s == 0 else adj1, s)
        y_up, y_down = y_copies(s)

        @pl.when(gx < n_gx - 1)
        def _():
            x_up.wait_send()

        @pl.when(gx > 0)
        def _():
            x_down.wait_send()

        @pl.when(gy < n_gy - 1)
        def _():
            y_up.wait_send()

        @pl.when(gy > 0)
        def _():
            y_down.wait_send()

        wait_sent(message_out.at[s], message_send.at[s])
        wait_sent(return_out.at[s], return_send.at[s])
    wait_sent(tag_out, tag_send)
    pltpu.make_async_copy(outbuf, source_hbm, out_sem).wait()


def last_product(source_ref, inv_ref, wells_ref, out_ref, rounded_ref):
    for i in range(source_ref.shape[0]):
        for c in range(0, source_ref.shape[2], 256):
            cut = slice(c, c + 256)
            out_ref[i, :, cut] = (-dot(inv_ref[i], source_ref[i, :, cut])).astype(BF16)

    @pl.when(pl.program_id(0) == 0)
    def _():
        rounded_ref[...] = wells_ref[...].astype(BF16)


def local(
    n_gx,
    n_gy,
    later_adjoint,
    coupling,
    inverse_diag,
    tile_mask,
    perf_cell,
    perf_slot,
    perf_live,
    perf_coef,
    well_gain,
    misfit,
):
    span_x, span_y, span_z, unknowns, columns = later_adjoint.shape
    tiles = span_x * span_y * span_z
    n = n_gx * n_gy
    slots = CAPACITY * n
    width = 2 * slots
    adj = later_adjoint.reshape(tiles, 3, 4, 16, columns)
    coup = jnp.swapaxes(coupling.reshape(tiles, 6, 192, 48), 2, 3)
    inv = inverse_diag.reshape(tiles, 192, 192)
    any_space = pl.BlockSpec(memory_space=pl.ANY)
    vmem = pl.BlockSpec(memory_space=pltpu.VMEM)
    smem = pl.BlockSpec(memory_space=pltpu.SMEM)
    dma = pltpu.SemaphoreType.DMA
    block = (n, 8, 128)
    face = (STEPS, span_x, span_y, span_z, 48, columns)
    source, wells = pl.pallas_call(
        functools.partial(kernel, n_gx, n_gy),
        out_shape=(
            jax.ShapeDtypeStruct((tiles, 192, columns), BF16),
            jax.ShapeDtypeStruct((STEPS, 24, columns), F32),
        ),
        in_specs=[any_space] * 3 + [smem, vmem, smem, vmem, vmem, smem, any_space],
        out_specs=(any_space, vmem),
        scratch_shapes=[
            pltpu.VMEM(adj.shape, BF16),
            pltpu.VMEM(adj.shape, BF16),
            pltpu.VMEM((tiles, 192, columns), BF16),
            pltpu.VMEM(coup.shape, BF16),
            pltpu.VMEM(inv.shape, BF16),
            pltpu.VMEM((STEPS, 32, columns), F32),
            pltpu.VMEM((2, 144, 192), BF16),
            pltpu.VMEM((tiles, width, 192), BF16),
            pltpu.VMEM((tiles, 192, 192), BF16),
            pltpu.VMEM((tiles, 192, width + 96), BF16),
            pltpu.VMEM((tiles, 192, columns), F32),
            pltpu.VMEM(face, BF16),
            pltpu.VMEM(face, BF16),
            pltpu.VMEM(face, BF16),
            pltpu.VMEM((STEPS, tiles, 3, 16, columns), BF16),
            pltpu.VMEM((STEPS, 2, span_x, span_z, 48, columns), BF16),
            pltpu.VMEM((width, columns), F32),
            pltpu.VMEM((width, columns), BF16),
            pltpu.VMEM(block, I32),
            pltpu.VMEM(block, I32),
            pltpu.VMEM((STEPS,) + block, F32),
            pltpu.VMEM((STEPS,) + block, F32),
            pltpu.VMEM((STEPS,) + block, F32),
            pltpu.VMEM((STEPS,) + block, F32),
            pltpu.VMEM((slots, 128), BF16),
            pltpu.VMEM((32, slots), BF16),
            dma((7,)),
            dma,
            dma((STEPS, 2)),
            dma((STEPS, 2)),
            dma((STEPS, 2)),
            dma((STEPS, 2)),
            dma,
            dma,
            dma((STEPS,)),
            dma((STEPS,)),
            dma((STEPS,)),
            dma((STEPS,)),
        ],
        compiler_params=pltpu.CompilerParams(
            collective_id=0, has_side_effects=True, vmem_limit_bytes=56 * 1024 * 1024
        ),
    )(
        adj,
        coup,
        inv,
        tile_mask,
        perf_cell,
        perf_slot,
        perf_live,
        perf_coef,
        well_gain,
        misfit,
    )
    pair = 2
    out, rounded = pl.pallas_call(
        last_product,
        grid=(tiles // pair,),
        out_shape=(
            jax.ShapeDtypeStruct((tiles, 192, columns), BF16),
            jax.ShapeDtypeStruct(wells.shape, BF16),
        ),
        in_specs=[
            pl.BlockSpec((pair, 192, columns), lambda i: (i, 0, 0)),
            pl.BlockSpec((pair, 192, 192), lambda i: (i, 0, 0)),
            pl.BlockSpec(wells.shape, lambda i: (0, 0, 0)),
        ],
        out_specs=(
            pl.BlockSpec((pair, 192, columns), lambda i: (i, 0, 0)),
            pl.BlockSpec(wells.shape, lambda i: (0, 0, 0)),
        ),
        compiler_params=pltpu.CompilerParams(vmem_limit_bytes=56 * 1024 * 1024),
    )(source, inv, wells)
    return out.reshape(later_adjoint.shape), rounded


def solution(mesh):
    return jax.shard_map(
        functools.partial(local, mesh.shape["gx"], mesh.shape["gy"]),
        mesh=mesh,
        in_specs=(
            P("gx", "gy", None, None, None),
            P("gx", "gy", None, None, None, None),
            P("gx", "gy", None, None, None),
            P("gx", "gy", None, None),
            P(("gx", "gy"), None),
            P(("gx", "gy"), None),
            P(("gx", "gy"), None),
            P(None, ("gx", "gy"), None),
            P(("gx", "gy")),
            P(None, ("gx", "gy"), None),
        ),
        out_specs=(P("gx", "gy", None, None, None), P(None, ("gx", "gy"), None)),
        check_vma=False,
    )
```

```python
import functools
import jax
import jax.numpy as jnp
from jax import lax
from jax.experimental import pallas as pl
from jax.experimental.pallas import tpu as pltpu
from jax.sharding import PartitionSpec as P

CAPACITY = 2
STEPS = 2
MESH = pl.DeviceIdType.MESH
BF16 = jnp.bfloat16
F32 = jnp.float32
I32 = jnp.int32


def dot(a, b):
    return jnp.dot(a, b, preferred_element_type=F32)


def iota(shape, dim):
    return lax.broadcasted_iota(I32, shape, dim)


def kernel(
    n_gx,
    n_gy,
    adj_hbm,
    coup_hbm,
    inv_hbm,
    mask_ref,
    cell_ref,
    slot_ref,
    live_ref,
    coef_ref,
    gain_ref,
    misfit_hbm,
    source_hbm,
    wells_ref,
    adj0,
    adj1,
    outbuf,
    coup,
    inv,
    misfit,
    sel_face,
    gather_w,
    near_w,
    far_w,
    flux,
    face_ylo,
    face_yhi,
    face_z,
    halo_x,
    halo_y,
    message_acc,
    landed_rows,
    tag_out,
    tag_mid,
    tag_in,
    message_out,
    message_mid,
    message_in,
    return_out,
    return_mid,
    return_in,
    sel_rows,
    sel_wells,
    load_sems,
    out_sem,
    x_send,
    x_recv,
    y_send,
    y_recv,
    tag_send,
    tag_recv,
    message_send,
    message_recv,
    return_send,
    return_recv,
):
    n = n_gx * n_gy
    slots = CAPACITY * n
    tiles = adj0.shape[0]
    span_y = face_z.shape[2]
    columns = adj0.shape[-1]
    lanes = 128
    chunks = columns // lanes
    piece = 256
    cuts = [slice(c, c + piece) for c in range(0, columns, piece)]
    gx = lax.axis_index("gx")
    gy = lax.axis_index("gy")
    me = gx * n_gy + gy

    quarter = tiles // 4
    loads = [
        pltpu.make_async_copy(
            adj_hbm.at[pl.ds(q * quarter, quarter)],
            adj0.at[pl.ds(q * quarter, quarter)],
            load_sems.at[q],
        )
        for q in range(4)
    ]
    load_coup = pltpu.make_async_copy(coup_hbm, coup, load_sems.at[4])
    load_inv = pltpu.make_async_copy(inv_hbm, inv, load_sems.at[5])
    load_misfit = pltpu.make_async_copy(misfit_hbm, misfit.at[:, pl.ds(0, 24)], load_sems.at[6])
    for load in loads + [load_coup, load_inv, load_misfit]:
        load.start()

    barrier = pltpu.get_barrier_semaphore()

    for d in range(1, n_gx):
        peer = (lax.rem(gx + d, n_gx), gy)
        pl.semaphore_signal(barrier, inc=1, device_id=peer, device_id_type=MESH)
    for d in range(1, n_gy):
        peer = (gx, lax.rem(gy + d, n_gy))
        pl.semaphore_signal(barrier, inc=1, device_id=peer, device_id_type=MESH)

    def fill_tag(p, carry):
        upper = iota((8, lanes), 0) < 4
        tag_out[p // n_gy, lax.rem(p, n_gy)] = jnp.where(upper, slot_ref[0, 2 * p], slot_ref[0, 2 * p + 1])
        return carry

    lax.fori_loop(0, n, fill_tag, 0)

    row = iota((48, 192), 0)
    col = iota((48, 192), 1)
    start_y = (row // 4) * 16 + row % 4
    pick_ylo = jnp.where(col == start_y, 1.0, 0.0).astype(BF16)
    pick_yhi = jnp.where(col == start_y + 12, 1.0, 0.0).astype(BF16)
    for z in range(2):
        sel_face[z, 0:48] = pick_ylo
        sel_face[z, 48:96] = pick_yhi
        sel_face[z, 96:144] = jnp.where(col == 4 * row + 3 * (1 - z), 1.0, 0.0).astype(BF16)

    cell_row = jnp.concatenate([cell_ref[...], cell_ref[...]], axis=1)
    parts = []
    for k in range(3):
        coef = coef_ref[k] * live_ref[...].astype(F32)
        high = coef.astype(BF16).astype(F32)
        low = (coef - high).astype(BF16).astype(F32)
        parts.append(jnp.concatenate([high, low], axis=1))
    width = 2 * slots
    cell_col = jnp.broadcast_to(cell_row, (lanes, width)).T
    cell_col = jnp.concatenate([cell_col, cell_col[:, 0:64]], axis=1)
    lane = iota((width, 192), 1)
    wide = [jnp.broadcast_to(part, (lanes, width)).T for part in parts]
    wide = [jnp.concatenate([w, w[:, 0:64]], axis=1) for w in wide]
    coef_cols = jnp.where(lane < 64, wide[0], jnp.where(lane < 128, wide[1], wide[2]))
    shifted_col = cell_col - lane % 64
    coef_rows = jnp.concatenate(
        [jnp.broadcast_to(part, (64, width)) for part in parts], axis=0
    )
    shifted_row = jnp.broadcast_to(cell_row, (192, width)) - iota((192, width), 0) % 64

    def place(t, carry):
        gather_w[t] = jnp.where(shifted_col == 64 * t, coef_cols, 0.0).astype(BF16)
        far_w[t, :, 0:width] = jnp.where(shifted_row == 64 * t, coef_rows, 0.0).astype(BF16)
        return carry

    lax.fori_loop(0, tiles, place, 0)
    misfit[:, 24:32] = jnp.zeros((STEPS, 8, columns), F32)

    half = tiles // 2

    @pl.when(gx == 0)
    def _():
        halo_x[:, 0:half] = jnp.zeros((STEPS, half) + halo_x.shape[2:], BF16)

    @pl.when(gx == n_gx - 1)
    def _():
        halo_x[:, half:tiles] = jnp.zeros((STEPS, half) + halo_x.shape[2:], BF16)

    @pl.when(gy == 0)
    def _():
        halo_y[:, 0] = jnp.zeros((STEPS,) + halo_y.shape[2:], BF16)

    @pl.when(gy == n_gy - 1)
    def _():
        halo_y[:, 1] = jnp.zeros((STEPS,) + halo_y.shape[2:], BF16)

    pl.semaphore_wait(barrier, n_gx + n_gy - 2)

    def spread_gx(part, target, send, recv):
        pltpu.make_async_copy(part(gx), target.at[gx], recv).start()
        for d in range(1, n_gx):
            j = lax.rem(gx + d, n_gx)
            pltpu.make_async_remote_copy(
                src_ref=part(j),
                dst_ref=target.at[gx],
                send_sem=send,
                recv_sem=recv,
                device_id=(j, gy),
                device_id_type=MESH,
            ).start()

    def spread_gy(part, target, send, recv):
        pltpu.make_async_copy(part(gy), target.at[gy], recv).start()
        for d in range(1, n_gy):
            j = lax.rem(gy + d, n_gy)
            pltpu.make_async_remote_copy(
                src_ref=part(j),
                dst_ref=target.at[gy],
                send_sem=send,
                recv_sem=recv,
                device_id=(gx, j),
                device_id_type=MESH,
            ).start()

    def wait_all(target, recv):
        pltpu.make_async_copy(target, target, recv).wait()

    spread_gx(lambda j: tag_out.at[j], tag_mid, tag_send.at[0], tag_recv.at[0])

    def x_copies(src, s):
        up = pltpu.make_async_remote_copy(
            src_ref=src.at[pl.ds(half, half), :, 3],
            dst_ref=halo_x.at[s, pl.ds(0, half)],
            send_sem=x_send.at[s, 0],
            recv_sem=x_recv.at[s, 0],
            device_id=(gx + 1, gy),
            device_id_type=MESH,
        )
        down = pltpu.make_async_remote_copy(
            src_ref=src.at[pl.ds(0, half), :, 0],
            dst_ref=halo_x.at[s, pl.ds(half, half)],
            send_sem=x_send.at[s, 1],
            recv_sem=x_recv.at[s, 1],
            device_id=(gx - 1, gy),
            device_id_type=MESH,
        )
        return up, down

    def y_copies(s):
        up = pltpu.make_async_remote_copy(
            src_ref=face_yhi.at[s, :, span_y - 1],
            dst_ref=halo_y.at[s, 0],
            send_sem=y_send.at[s, 0],
            recv_sem=y_recv.at[s, 0],
            device_id=(gx, gy + 1),
            device_id_type=MESH,
        )
        down = pltpu.make_async_remote_copy(
            src_ref=face_ylo.at[s, :, 0],
            dst_ref=halo_y.at[s, 1],
            send_sem=y_send.at[s, 1],
            recv_sem=y_recv.at[s, 1],
            device_id=(gx, gy - 1),
            device_id_type=MESH,
        )
        return up, down

    def for_pairs(y, body):
        for x in range(2):
            for z in range(2):
                body(x, z, (x * span_y + y) * 2 + z)

    y_order = [0, span_y - 1] + list(range(1, span_y - 1))

    def start_x(src, s):
        x_up, x_down = x_copies(src, s)

        @pl.when(gx < n_gx - 1)
        def _():
            x_up.start()

        @pl.when(gx > 0)
        def _():
            x_down.start()

    def faces(src, s, y):
        y_up, y_down = y_copies(s)

        def body(x, z, t):
            for cut in cuts:
                whole = src[t, :, :, :, cut].reshape(192, piece)
                got = dot(sel_face[z], whole)
                face_ylo[s, x, y, z, :, cut] = got[0:48].astype(BF16)
                face_yhi[s, x, y, z, :, cut] = got[48:96].astype(BF16)
                face_z[s, x, y, z, :, cut] = got[96:144].astype(BF16)
                term = dot(gather_w[t], whole)
                if y == 0 and x == 0 and z == 0:
                    message_acc[:, cut] = term
                else:
                    message_acc[:, cut] += term

        for_pairs(y, body)
        if y == 0:

            @pl.when(gy > 0)
            def _():
                y_down.start()

        if y == span_y - 1:

            @pl.when(gy < n_gy - 1)
            def _():
                y_up.start()

    for load in loads:
        load.wait()
    start_x(adj0, 0)
    for y in y_order:
        faces(adj0, 0, y)
        if y == span_y - 1:
            wait_all(tag_mid, tag_recv.at[0])
            spread_gy(lambda j: tag_mid.at[:, j], tag_in, tag_send.at[1], tag_recv.at[1])

    for s in range(STEPS):
        src = adj0 if s == 0 else adj1
        x_up, x_down = x_copies(src, s)
        y_up, y_down = y_copies(s)

        message = message_acc[0:slots] + message_acc[slots:width]
        message = message.astype(BF16).astype(F32)
        for q in range(chunks):
            flat = message_out.at[s].reshape(n * 8, lanes)
            flat[pl.ds(q, slots, stride=chunks), :] = message[:, q * lanes : (q + 1) * lanes]
        spread_gx(
            lambda j: message_out.at[s, j],
            message_mid.at[s],
            message_send.at[s, 0],
            message_recv.at[s, 0],
        )

        if s == 0:
            load_coup.wait()

            def weights(y):
                def body(x, z, t):
                    def block(d):
                        keep = mask_ref[x, y, z, d] != 0
                        return jnp.where(keep, coup[t, d], jnp.zeros((48, 192), BF16))

                    near = [block(1 - x), block(5 - z)]
                    far = [block(x)]
                    (near if y > 0 else far).append(block(2))
                    (near if y < span_y - 1 else far).append(block(3))
                    near_w[t, :, 0 : 48 * len(near)] = jnp.concatenate(near, axis=0).T
                    far_w[t, :, width : width + 48 * len(far)] = jnp.concatenate(far, axis=0).T

                for_pairs(y, body)

        def near_flux(y):
            if s == 0:
                weights(y)

            def body(x, z, t):
                beside = ((1 - x) * span_y + y) * 2 + z
                for cut in cuts:
                    listed = [src[beside, :, 3 * x, :, cut].reshape(48, piece)]
                    listed.append(face_z[s, x, y, 1 - z, :, cut])
                    if y > 0:
                        listed.append(face_yhi[s, x, y - 1, z, :, cut])
                    if y < span_y - 1:
                        listed.append(face_ylo[s, x, y + 1, z, :, cut])
                    depth = 48 * len(listed)
                    flux[t, :, cut] = dot(near_w[t, :, 0:depth], jnp.concatenate(listed, axis=0))

            for_pairs(y, body)

        near_flux(0)
        wait_all(message_mid.at[s], message_recv.at[s, 0])
        spread_gy(
            lambda j: message_mid.at[s, :, j],
            message_in.at[s],
            message_send.at[s, 1],
            message_recv.at[s, 1],
        )
        near_flux(span_y - 1)

        if s == 0:
            load_misfit.wait()
            wait_all(tag_in, tag_recv.at[1])
            tags = tag_in.reshape(n * 8, lanes)[pl.ds(0, slots, stride=4), :]
            chosen = jnp.where(tags == iota((slots, lanes), 1), 1.0, 0.0)
            sel_rows[...] = chosen.astype(BF16)
            sel_wells[...] = chosen.T[0:32].astype(BF16)
        wait_all(message_in.at[s], message_recv.at[s, 1])
        flat_in = message_in.at[s].reshape(n * 8, lanes)
        arrived = jnp.concatenate(
            [flat_in[pl.ds(q, slots, stride=chunks), :] for q in range(chunks)], axis=1
        ).astype(BF16)
        gain_row = iota((32, 1), 0)
        gain = jnp.zeros((32, 1), F32)
        for w in range(24):
            gain = jnp.where(gain_row == w, gain_ref[w], gain)
        well = (gain * (dot(sel_wells[...], arrived) + misfit[s])).astype(BF16)
        wells_ref[s] = well.astype(F32)[0:24]
        returned = dot(sel_rows[:, 0:32], well)
        flat_out = return_out.at[s].reshape(n * 8, lanes)
        for q in range(chunks):
            flat_out[pl.ds(q, slots, stride=chunks), :] = returned[:, q * lanes : (q + 1) * lanes]
        spread_gy(
            lambda j: return_out.at[s, j],
            return_mid.at[s],
            return_send.at[s, 0],
            return_recv.at[s, 0],
        )
        for y in range(1, span_y // 2):
            near_flux(y)
        wait_all(return_mid.at[s], return_recv.at[s, 0])
        spread_gx(
            lambda j: return_mid.at[s, :, j],
            return_in.at[s],
            return_send.at[s, 1],
            return_recv.at[s, 1],
        )
        for y in range(span_y // 2, span_y - 1):
            near_flux(y)

        @pl.when(gx > 0)
        def _():
            x_up.wait_recv()

        @pl.when(gx < n_gx - 1)
        def _():
            x_down.wait_recv()

        @pl.when(gy > 0)
        def _():
            y_up.wait_recv()

        @pl.when(gy < n_gy - 1)
        def _():
            y_down.wait_recv()

        if s == 0:
            load_inv.wait()
        wait_all(return_in.at[s], return_recv.at[s, 1])
        flat_back = return_in.at[s].reshape(n * 8, lanes)
        landed = jnp.concatenate(
            [flat_back[pl.ds(q, slots, stride=chunks), :] for q in range(chunks)], axis=1
        ).astype(BF16)
        landed_rows[0:slots] = landed
        landed_rows[slots:width] = landed

        def far_source(y, x, z, cut):
            t = (x * span_y + y) * 2 + z
            listed = [landed_rows[:, cut], halo_x[s, t, :, :, cut].reshape(48, piece)]
            if y == 0:
                listed.append(halo_y[s, 0, x, z, :, cut])
            if y == span_y - 1:
                listed.append(halo_y[s, 1, x, z, :, cut])
            depth = width + 48 * (len(listed) - 1)
            added = dot(far_w[t, :, 0:depth], jnp.concatenate(listed, axis=0))
            return (flux[t, :, cut] + added).astype(BF16)

        for y in y_order:
            items = [(x, z, cut) for x in range(2) for z in range(2) for cut in cuts]
            ready = far_source(y, *items[0])
            for i, (x, z, cut) in enumerate(items):
                t = (x * span_y + y) * 2 + z
                source = ready
                if i + 1 < len(items):
                    ready = far_source(y, *items[i + 1])
                if s < STEPS - 1:
                    new = (-dot(inv[t], source)).astype(BF16)
                    adj1[t, :, :, :, cut] = new.reshape(3, 4, 16, piece)
                else:
                    outbuf[t, :, cut] = source
            if s < STEPS - 1:
                if y == y_order[-1]:
                    start_x(adj1, s + 1)
                faces(adj1, s + 1, y)
            else:
                for x in range(2):
                    rows = pl.ds((x * span_y + y) * 2, 2)
                    pltpu.make_async_copy(outbuf.at[rows], source_hbm.at[rows], out_sem).start()

    for s in range(STEPS):
        x_up, x_down = x_copies(adj0 if s == 0 else adj1, s)
        y_up, y_down = y_copies(s)

        @pl.when(gx < n_gx - 1)
        def _():
            x_up.wait_send()

        @pl.when(gx > 0)
        def _():
            x_down.wait_send()

        @pl.when(gy < n_gy - 1)
        def _():
            y_up.wait_send()

        @pl.when(gy > 0)
        def _():
            y_down.wait_send()

        wait_all(message_out.at[s, pl.ds(0, n_gx - 1)], message_send.at[s, 0])
        wait_all(message_mid.at[s, :, pl.ds(0, n_gy - 1)], message_send.at[s, 1])
        wait_all(return_out.at[s, pl.ds(0, n_gy - 1)], return_send.at[s, 0])
        wait_all(return_mid.at[s, :, pl.ds(0, n_gx - 1)], return_send.at[s, 1])
    wait_all(tag_out.at[pl.ds(0, n_gx - 1)], tag_send.at[0])
    wait_all(tag_mid.at[:, pl.ds(0, n_gy - 1)], tag_send.at[1])
    pltpu.make_async_copy(outbuf, source_hbm, out_sem).wait()


def last_product(
    source_hbm, inv_hbm, wells_hbm, out_hbm, rounded_ref, source, inv, wells, out, in_sems, wells_sem, out_sem
):
    tiles = source.shape[0]
    group = 2
    loads = []
    for g in range(tiles // group):
        rows = pl.ds(g * group, group)
        pair = (
            pltpu.make_async_copy(inv_hbm.at[rows], inv.at[rows], in_sems.at[g, 0]),
            pltpu.make_async_copy(source_hbm.at[rows], source.at[rows], in_sems.at[g, 1]),
        )
        for load in pair:
            load.start()
        loads.append(pair)
    load_wells = pltpu.make_async_copy(wells_hbm, wells, wells_sem)
    load_wells.start()
    for g, pair in enumerate(loads):
        for load in pair:
            load.wait()
        for t in range(g * group, (g + 1) * group):
            for c in range(0, source.shape[2], 256):
                cut = slice(c, c + 256)
                out[t, :, cut] = (-dot(inv[t], source[t, :, cut])).astype(BF16)
        rows = pl.ds(g * group, group)
        pltpu.make_async_copy(out.at[rows], out_hbm.at[rows], out_sem).start()
    load_wells.wait()
    rounded_ref[...] = wells[...].astype(BF16)
    pltpu.make_async_copy(out, out_hbm, out_sem).wait()


def local(
    n_gx,
    n_gy,
    later_adjoint,
    coupling,
    inverse_diag,
    tile_mask,
    perf_cell,
    perf_slot,
    perf_live,
    perf_coef,
    well_gain,
    misfit,
):
    span_x, span_y, span_z, unknowns, columns = later_adjoint.shape
    tiles = span_x * span_y * span_z
    n = n_gx * n_gy
    slots = CAPACITY * n
    width = 2 * slots
    adj = later_adjoint.reshape(tiles, 3, 4, 16, columns)
    coup = jnp.swapaxes(coupling.reshape(tiles, 6, 192, 48), 2, 3)
    inv = inverse_diag.reshape(tiles, 192, 192)
    any_space = pl.BlockSpec(memory_space=pl.ANY)
    vmem = pl.BlockSpec(memory_space=pltpu.VMEM)
    smem = pl.BlockSpec(memory_space=pltpu.SMEM)
    dma = pltpu.SemaphoreType.DMA
    by_gx = (n_gx, n_gy, 8, 128)
    by_gy = (n_gy, n_gx, 8, 128)
    face = (STEPS, span_x, span_y, span_z, 48, columns)
    source, wells = pl.pallas_call(
        functools.partial(kernel, n_gx, n_gy),
        out_shape=(
            jax.ShapeDtypeStruct((tiles, 192, columns), BF16),
            jax.ShapeDtypeStruct((STEPS, 24, columns), F32),
        ),
        in_specs=[any_space] * 3 + [smem, vmem, smem, vmem, vmem, smem, any_space],
        out_specs=(any_space, vmem),
        scratch_shapes=[
            pltpu.VMEM(adj.shape, BF16),
            pltpu.VMEM(adj.shape, BF16),
            pltpu.VMEM((tiles, 192, columns), BF16),
            pltpu.VMEM(coup.shape, BF16),
            pltpu.VMEM(inv.shape, BF16),
            pltpu.VMEM((STEPS, 32, columns), F32),
            pltpu.VMEM((2, 144, 192), BF16),
            pltpu.VMEM((tiles, width, 192), BF16),
            pltpu.VMEM((tiles, 192, 192), BF16),
            pltpu.VMEM((tiles, 192, width + 96), BF16),
            pltpu.VMEM((tiles, 192, columns), F32),
            pltpu.VMEM(face, BF16),
            pltpu.VMEM(face, BF16),
            pltpu.VMEM(face, BF16),
            pltpu.VMEM((STEPS, tiles, 3, 16, columns), BF16),
            pltpu.VMEM((STEPS, 2, span_x, span_z, 48, columns), BF16),
            pltpu.VMEM((width, columns), F32),
            pltpu.VMEM((width, columns), BF16),
            pltpu.VMEM(by_gx, I32),
            pltpu.VMEM(by_gx, I32),
            pltpu.VMEM(by_gy, I32),
            pltpu.VMEM((STEPS,) + by_gx, F32),
            pltpu.VMEM((STEPS,) + by_gx, F32),
            pltpu.VMEM((STEPS,) + by_gy, F32),
            pltpu.VMEM((STEPS,) + by_gy, F32),
            pltpu.VMEM((STEPS,) + by_gy, F32),
            pltpu.VMEM((STEPS,) + by_gx, F32),
            pltpu.VMEM((slots, 128), BF16),
            pltpu.VMEM((32, slots), BF16),
            dma((7,)),
            dma,
            dma((STEPS, 2)),
            dma((STEPS, 2)),
            dma((STEPS, 2)),
            dma((STEPS, 2)),
            dma((2,)),
            dma((2,)),
            dma((STEPS, 2)),
            dma((STEPS, 2)),
            dma((STEPS, 2)),
            dma((STEPS, 2)),
        ],
        compiler_params=pltpu.CompilerParams(
            collective_id=0, has_side_effects=True, vmem_limit_bytes=56 * 1024 * 1024
        ),
    )(
        adj,
        coup,
        inv,
        tile_mask,
        perf_cell,
        perf_slot,
        perf_live,
        perf_coef,
        well_gain,
        misfit,
    )
    out, rounded = pl.pallas_call(
        last_product,
        out_shape=(
            jax.ShapeDtypeStruct((tiles, 192, columns), BF16),
            jax.ShapeDtypeStruct(wells.shape, BF16),
        ),
        in_specs=[any_space] * 3,
        out_specs=(any_space, vmem),
        scratch_shapes=[
            pltpu.VMEM((tiles, 192, columns), BF16),
            pltpu.VMEM((tiles, 192, 192), BF16),
            pltpu.VMEM(wells.shape, F32),
            pltpu.VMEM((tiles, 192, columns), BF16),
            dma((tiles // 2, 2)),
            dma,
            dma,
        ],
        compiler_params=pltpu.CompilerParams(vmem_limit_bytes=56 * 1024 * 1024),
    )(source, inv, wells)
    return out.reshape(later_adjoint.shape), rounded


def solution(mesh):
    return jax.shard_map(
        functools.partial(local, mesh.shape["gx"], mesh.shape["gy"]),
        mesh=mesh,
        in_specs=(
            P("gx", "gy", None, None, None),
            P("gx", "gy", None, None, None, None),
            P("gx", "gy", None, None, None),
            P("gx", "gy", None, None),
            P(("gx", "gy"), None),
            P(("gx", "gy"), None),
            P(("gx", "gy"), None),
            P(None, ("gx", "gy"), None),
            P(("gx", "gy")),
            P(None, ("gx", "gy"), None),
        ),
        out_specs=(P("gx", "gy", None, None, None), P(None, ("gx", "gy"), None)),
        check_vma=False,
    )
```

```python
import functools
import jax
import jax.numpy as jnp
from jax import lax
from jax.experimental import pallas as pl
from jax.experimental.pallas import tpu as pltpu
from jax.sharding import PartitionSpec as P

CAPACITY = 2
STEPS = 2
MESH = pl.DeviceIdType.MESH
BF16 = jnp.bfloat16
F32 = jnp.float32
I32 = jnp.int32


def dot(a, b):
    return jnp.dot(a, b, preferred_element_type=F32)


def iota(shape, dim):
    return lax.broadcasted_iota(I32, shape, dim)


def kernel(
    n_gx,
    n_gy,
    adj_hbm,
    coup_hbm,
    inv_hbm,
    mask_ref,
    cell_ref,
    slot_ref,
    live_ref,
    coef_ref,
    gain_ref,
    misfit_hbm,
    source_hbm,
    wells_ref,
    adj0,
    adj1,
    outbuf,
    coup,
    inv,
    misfit,
    sel_face,
    gather_w,
    near_w,
    far_w,
    flux,
    face_ylo,
    face_yhi,
    face_z,
    halo_x,
    halo_y,
    message_acc,
    landed_rows,
    tag_out,
    tag_in,
    message_out,
    message_in,
    return_out,
    return_in,
    stage,
    sel_rows,
    sel_wells,
    load_sems,
    out_sem,
    x_send,
    x_recv,
    y_send,
    y_recv,
    tag_send,
    tag_recv,
    message_send,
    message_recv,
    return_send,
    return_recv,
):
    n = n_gx * n_gy
    slots = CAPACITY * n
    tiles = adj0.shape[0]
    span_y = face_z.shape[2]
    columns = adj0.shape[-1]
    lanes = 128
    chunks = columns // lanes
    piece = 256
    cuts = [slice(c, c + piece) for c in range(0, columns, piece)]
    gx = lax.axis_index("gx")
    gy = lax.axis_index("gy")
    me = gx * n_gy + gy

    quarter = tiles // 4
    loads = [
        pltpu.make_async_copy(
            adj_hbm.at[pl.ds(q * quarter, quarter)],
            adj0.at[pl.ds(q * quarter, quarter)],
            load_sems.at[q],
        )
        for q in range(4)
    ]
    load_coup = pltpu.make_async_copy(coup_hbm, coup, load_sems.at[4])
    load_inv = pltpu.make_async_copy(inv_hbm, inv, load_sems.at[5])
    load_misfit = pltpu.make_async_copy(misfit_hbm, misfit.at[:, pl.ds(0, 24)], load_sems.at[6])
    for load in loads + [load_coup, load_inv, load_misfit]:
        load.start()

    barrier = pltpu.get_barrier_semaphore()

    def greet(d, carry):
        j = lax.rem(me + d, n)
        pl.semaphore_signal(
            barrier, inc=1, device_id=(j // n_gy, lax.rem(j, n_gy)), device_id_type=MESH
        )
        return carry

    lax.fori_loop(1, n, greet, 0)

    def fill_tag(p, carry):
        upper = iota((8, lanes), 0) < 4
        tag_out[p] = jnp.where(upper, slot_ref[0, 2 * p], slot_ref[0, 2 * p + 1]).astype(F32).astype(BF16)
        return carry

    lax.fori_loop(0, n, fill_tag, 0)

    row = iota((48, 192), 0)
    col = iota((48, 192), 1)
    start_y = (row // 4) * 16 + row % 4
    pick_ylo = jnp.where(col == start_y, 1.0, 0.0).astype(BF16)
    pick_yhi = jnp.where(col == start_y + 12, 1.0, 0.0).astype(BF16)
    for z in range(2):
        sel_face[z, 0:48] = pick_ylo
        sel_face[z, 48:96] = pick_yhi
        sel_face[z, 96:144] = jnp.where(col == 4 * row + 3 * (1 - z), 1.0, 0.0).astype(BF16)

    cell_row = jnp.concatenate([cell_ref[...], cell_ref[...]], axis=1)
    parts = []
    for k in range(3):
        coef = coef_ref[k] * live_ref[...].astype(F32)
        high = coef.astype(BF16).astype(F32)
        low = (coef - high).astype(BF16).astype(F32)
        parts.append(jnp.concatenate([high, low], axis=1))
    width = 2 * slots
    cell_col = jnp.broadcast_to(cell_row, (lanes, width)).T
    cell_col = jnp.concatenate([cell_col, cell_col[:, 0:64]], axis=1)
    lane = iota((width, 192), 1)
    wide = [jnp.broadcast_to(part, (lanes, width)).T for part in parts]
    wide = [jnp.concatenate([w, w[:, 0:64]], axis=1) for w in wide]
    coef_cols = jnp.where(lane < 64, wide[0], jnp.where(lane < 128, wide[1], wide[2]))
    shifted_col = cell_col - lane % 64
    coef_rows = jnp.concatenate(
        [jnp.broadcast_to(part, (64, width)) for part in parts], axis=0
    )
    shifted_row = jnp.broadcast_to(cell_row, (192, width)) - iota((192, width), 0) % 64

    def place(t, carry):
        gather_w[t] = jnp.where(shifted_col == 64 * t, coef_cols, 0.0).astype(BF16)
        far_w[t, :, 0:width] = jnp.where(shifted_row == 64 * t, coef_rows, 0.0).astype(BF16)
        return carry

    lax.fori_loop(0, tiles, place, 0)
    misfit[:, 24:32] = jnp.zeros((STEPS, 8, columns), F32)

    half = tiles // 2

    @pl.when(gx == 0)
    def _():
        halo_x[:, 0:half] = jnp.zeros((STEPS, half) + halo_x.shape[2:], BF16)

    @pl.when(gx == n_gx - 1)
    def _():
        halo_x[:, half:tiles] = jnp.zeros((STEPS, half) + halo_x.shape[2:], BF16)

    @pl.when(gy == 0)
    def _():
        halo_y[:, 0] = jnp.zeros((STEPS,) + halo_y.shape[2:], BF16)

    @pl.when(gy == n_gy - 1)
    def _():
        halo_y[:, 1] = jnp.zeros((STEPS,) + halo_y.shape[2:], BF16)

    pl.semaphore_wait(barrier, n - 1)

    def spread(source, target, send, recv):
        own = pltpu.make_async_copy(source.at[me], target.at[me], recv)
        own.start()

        def one(d, carry):
            j = lax.rem(me + d, n)
            pltpu.make_async_remote_copy(
                src_ref=source.at[j],
                dst_ref=target.at[me],
                send_sem=send,
                recv_sem=recv,
                device_id=(j // n_gy, lax.rem(j, n_gy)),
                device_id_type=MESH,
            ).start()
            return carry

        lax.fori_loop(1, n, one, 0)

    def wait_all(target, recv):
        pltpu.make_async_copy(target, target, recv).wait()

    def wait_sent(source, send):
        part = source.at[pl.ds(0, n - 1)]
        pltpu.make_async_copy(part, part, send).wait()

    spread(tag_out, tag_in, tag_send, tag_recv)

    def x_copies(src, s, y):
        up = pltpu.make_async_remote_copy(
            src_ref=src.at[pl.ds(half + 2 * y, 2), :, 3],
            dst_ref=halo_x.at[s, pl.ds(2 * y, 2)],
            send_sem=x_send.at[s, y, 0],
            recv_sem=x_recv.at[s, y, 0],
            device_id=(gx + 1, gy),
            device_id_type=MESH,
        )
        down = pltpu.make_async_remote_copy(
            src_ref=src.at[pl.ds(2 * y, 2), :, 0],
            dst_ref=halo_x.at[s, pl.ds(half + 2 * y, 2)],
            send_sem=x_send.at[s, y, 1],
            recv_sem=x_recv.at[s, y, 1],
            device_id=(gx - 1, gy),
            device_id_type=MESH,
        )
        return up, down

    def y_copies(s):
        up = pltpu.make_async_remote_copy(
            src_ref=face_yhi.at[s, :, span_y - 1],
            dst_ref=halo_y.at[s, 0],
            send_sem=y_send.at[s, 0],
            recv_sem=y_recv.at[s, 0],
            device_id=(gx, gy + 1),
            device_id_type=MESH,
        )
        down = pltpu.make_async_remote_copy(
            src_ref=face_ylo.at[s, :, 0],
            dst_ref=halo_y.at[s, 1],
            send_sem=y_send.at[s, 1],
            recv_sem=y_recv.at[s, 1],
            device_id=(gx, gy - 1),
            device_id_type=MESH,
        )
        return up, down

    def for_pairs(y, body):
        for x in range(2):
            for z in range(2):
                body(x, z, (x * span_y + y) * 2 + z)

    y_order = [0, span_y - 1] + list(range(1, span_y - 1))

    def start_x(src, s, y):
        x_up, x_down = x_copies(src, s, y)

        @pl.when(gx < n_gx - 1)
        def _():
            x_up.start()

        @pl.when(gx > 0)
        def _():
            x_down.start()

    def faces(src, s, y):
        y_up, y_down = y_copies(s)

        def body(x, z, t):
            for cut in cuts:
                whole = src[t, :, :, :, cut].reshape(192, piece)
                got = dot(sel_face[z], whole)
                face_ylo[s, x, y, z, :, cut] = got[0:48].astype(BF16)
                face_yhi[s, x, y, z, :, cut] = got[48:96].astype(BF16)
                face_z[s, x, y, z, :, cut] = got[96:144].astype(BF16)
                term = dot(gather_w[t], whole)
                if y == 0 and x == 0 and z == 0:
                    message_acc[:, cut] = term
                else:
                    message_acc[:, cut] += term

        for_pairs(y, body)
        if y == 0:

            @pl.when(gy > 0)
            def _():
                y_down.start()

        if y == span_y - 1:

            @pl.when(gy < n_gy - 1)
            def _():
                y_up.start()

    for load in loads:
        load.wait()
    for y in y_order:
        start_x(adj0, 0, y)
        faces(adj0, 0, y)

    for s in range(STEPS):
        src = adj0 if s == 0 else adj1
        y_up, y_down = y_copies(s)

        message = message_acc[0:slots] + message_acc[slots:width]
        message = message.astype(BF16).astype(F32)
        for q in range(chunks):
            stage[pl.ds(q, slots, stride=chunks), :] = message[:, q * lanes : (q + 1) * lanes]
        message_out[s] = stage[...].reshape(n, 8, lanes).astype(BF16)
        spread(message_out.at[s], message_in.at[s], message_send.at[s], message_recv.at[s])

        if s == 0:
            load_coup.wait()

            def weights(y):
                def body(x, z, t):
                    def block(d):
                        keep = mask_ref[x, y, z, d] != 0
                        return jnp.where(keep, coup[t, d], jnp.zeros((48, 192), BF16))

                    near = [block(1 - x), block(5 - z)]
                    far = [block(x)]
                    (near if y > 0 else far).append(block(2))
                    (near if y < span_y - 1 else far).append(block(3))
                    near_w[t, :, 0 : 48 * len(near)] = jnp.concatenate(near, axis=0).T
                    far_w[t, :, width : width + 48 * len(far)] = jnp.concatenate(far, axis=0).T

                for_pairs(y, body)

            for y in range(span_y):
                weights(y)

        def near_flux(y):
            def body(x, z, t):
                beside = ((1 - x) * span_y + y) * 2 + z
                for cut in cuts:
                    listed = [src[beside, :, 3 * x, :, cut].reshape(48, piece)]
                    listed.append(face_z[s, x, y, 1 - z, :, cut])
                    if y > 0:
                        listed.append(face_yhi[s, x, y - 1, z, :, cut])
                    if y < span_y - 1:
                        listed.append(face_ylo[s, x, y + 1, z, :, cut])
                    depth = 48 * len(listed)
                    flux[t, :, cut] = dot(near_w[t, :, 0:depth], jnp.concatenate(listed, axis=0))

            for_pairs(y, body)

        for y in range(span_y):
            near_flux(y)

        if s == 0:
            load_misfit.wait()
            wait_all(tag_in, tag_recv)
            stage[...] = tag_in[...].astype(F32).reshape(n * 8, lanes)
            tags = stage[pl.ds(0, slots, stride=4), :]
            chosen = jnp.where(tags.astype(I32) == iota((slots, lanes), 1), 1.0, 0.0)
            sel_rows[...] = chosen.astype(BF16)
            sel_wells[...] = chosen.T[0:32].astype(BF16)
        wait_all(message_in.at[s], message_recv.at[s])
        stage[...] = message_in[s].astype(F32).reshape(n * 8, lanes)
        arrived = jnp.concatenate(
            [stage[pl.ds(q, slots, stride=chunks), :] for q in range(chunks)], axis=1
        ).astype(BF16)
        gain_row = iota((32, 1), 0)
        gain = jnp.zeros((32, 1), F32)
        for w in range(24):
            gain = jnp.where(gain_row == w, gain_ref[w], gain)
        well = (gain * (dot(sel_wells[...], arrived) + misfit[s])).astype(BF16)
        wells_ref[s] = well.astype(F32)[0:24]
        returned = dot(sel_rows[:, 0:32], well)
        for q in range(chunks):
            stage[pl.ds(q, slots, stride=chunks), :] = returned[:, q * lanes : (q + 1) * lanes]
        return_out[s] = stage[...].reshape(n, 8, lanes).astype(BF16)
        spread(return_out.at[s], return_in.at[s], return_send.at[s], return_recv.at[s])

        if s == 0:
            load_inv.wait()
        wait_all(return_in.at[s], return_recv.at[s])
        stage[...] = return_in[s].astype(F32).reshape(n * 8, lanes)
        landed = jnp.concatenate(
            [stage[pl.ds(q, slots, stride=chunks), :] for q in range(chunks)], axis=1
        ).astype(BF16)
        landed_rows[0:slots] = landed
        landed_rows[slots:width] = landed

        def far_source(y, x, z, cut):
            t = (x * span_y + y) * 2 + z
            listed = [landed_rows[:, cut], halo_x[s, t, :, :, cut].reshape(48, piece)]
            if y == 0:
                listed.append(halo_y[s, 0, x, z, :, cut])
            if y == span_y - 1:
                listed.append(halo_y[s, 1, x, z, :, cut])
            depth = width + 48 * (len(listed) - 1)
            added = dot(far_w[t, :, 0:depth], jnp.concatenate(listed, axis=0))
            return (flux[t, :, cut] + added).astype(BF16)

        for y in y_order:
            x_up, x_down = x_copies(src, s, y)

            @pl.when(gx > 0)
            def _():
                x_up.wait_recv()

            @pl.when(gx < n_gx - 1)
            def _():
                x_down.wait_recv()

            if y == 0:

                @pl.when(gy > 0)
                def _():
                    y_up.wait_recv()

            if y == span_y - 1:

                @pl.when(gy < n_gy - 1)
                def _():
                    y_down.wait_recv()

            items = [(x, z, cut) for x in range(2) for z in range(2) for cut in cuts]
            ready = far_source(y, *items[0])
            for i, (x, z, cut) in enumerate(items):
                t = (x * span_y + y) * 2 + z
                source = ready
                if i + 1 < len(items):
                    ready = far_source(y, *items[i + 1])
                if s < STEPS - 1:
                    new = (-dot(inv[t], source)).astype(BF16)
                    adj1[t, :, :, :, cut] = new.reshape(3, 4, 16, piece)
                else:
                    outbuf[t, :, cut] = source
            if s < STEPS - 1:
                start_x(adj1, s + 1, y)
                faces(adj1, s + 1, y)
            else:
                for x in range(2):
                    rows = pl.ds((x * span_y + y) * 2, 2)
                    pltpu.make_async_copy(outbuf.at[rows], source_hbm.at[rows], out_sem).start()

    for s in range(STEPS):
        y_up, y_down = y_copies(s)
        for y in range(span_y):
            x_up, x_down = x_copies(adj0 if s == 0 else adj1, s, y)

            @pl.when(gx < n_gx - 1)
            def _():
                x_up.wait_send()

            @pl.when(gx > 0)
            def _():
                x_down.wait_send()

        @pl.when(gy < n_gy - 1)
        def _():
            y_up.wait_send()

        @pl.when(gy > 0)
        def _():
            y_down.wait_send()

        wait_sent(message_out.at[s], message_send.at[s])
        wait_sent(return_out.at[s], return_send.at[s])
    wait_sent(tag_out, tag_send)
    pltpu.make_async_copy(outbuf, source_hbm, out_sem).wait()


def last_product(
    source_hbm, inv_hbm, wells_hbm, out_hbm, rounded_ref, source, inv, wells, out, in_sems, wells_sem, out_sem
):
    tiles = source.shape[0]
    group = 2
    loads = []
    for g in range(tiles // group):
        rows = pl.ds(g * group, group)
        pair = (
            pltpu.make_async_copy(inv_hbm.at[rows], inv.at[rows], in_sems.at[g, 0]),
            pltpu.make_async_copy(source_hbm.at[rows], source.at[rows], in_sems.at[g, 1]),
        )
        for load in pair:
            load.start()
        loads.append(pair)
    load_wells = pltpu.make_async_copy(wells_hbm, wells, wells_sem)
    load_wells.start()
    for g, pair in enumerate(loads):
        for load in pair:
            load.wait()
        for t in range(g * group, (g + 1) * group):
            for c in range(0, source.shape[2], 256):
                cut = slice(c, c + 256)
                out[t, :, cut] = (-dot(inv[t], source[t, :, cut])).astype(BF16)
        rows = pl.ds(g * group, group)
        pltpu.make_async_copy(out.at[rows], out_hbm.at[rows], out_sem).start()
    load_wells.wait()
    rounded_ref[...] = wells[...].astype(BF16)
    pltpu.make_async_copy(out, out_hbm, out_sem).wait()


def local(
    n_gx,
    n_gy,
    later_adjoint,
    coupling,
    inverse_diag,
    tile_mask,
    perf_cell,
    perf_slot,
    perf_live,
    perf_coef,
    well_gain,
    misfit,
):
    span_x, span_y, span_z, unknowns, columns = later_adjoint.shape
    tiles = span_x * span_y * span_z
    n = n_gx * n_gy
    slots = CAPACITY * n
    width = 2 * slots
    adj = later_adjoint.reshape(tiles, 3, 4, 16, columns)
    coup = jnp.swapaxes(coupling.reshape(tiles, 6, 192, 48), 2, 3)
    inv = inverse_diag.reshape(tiles, 192, 192)
    any_space = pl.BlockSpec(memory_space=pl.ANY)
    vmem = pl.BlockSpec(memory_space=pltpu.VMEM)
    smem = pl.BlockSpec(memory_space=pltpu.SMEM)
    dma = pltpu.SemaphoreType.DMA
    block = (n, 8, 128)
    face = (STEPS, span_x, span_y, span_z, 48, columns)
    source, wells = pl.pallas_call(
        functools.partial(kernel, n_gx, n_gy),
        out_shape=(
            jax.ShapeDtypeStruct((tiles, 192, columns), BF16),
            jax.ShapeDtypeStruct((STEPS, 24, columns), F32),
        ),
        in_specs=[any_space] * 3 + [smem, vmem, smem, vmem, vmem, smem, any_space],
        out_specs=(any_space, vmem),
        scratch_shapes=[
            pltpu.VMEM(adj.shape, BF16),
            pltpu.VMEM(adj.shape, BF16),
            pltpu.VMEM((tiles, 192, columns), BF16),
            pltpu.VMEM(coup.shape, BF16),
            pltpu.VMEM(inv.shape, BF16),
            pltpu.VMEM((STEPS, 32, columns), F32),
            pltpu.VMEM((2, 144, 192), BF16),
            pltpu.VMEM((tiles, width, 192), BF16),
            pltpu.VMEM((tiles, 192, 192), BF16),
            pltpu.VMEM((tiles, 192, width + 96), BF16),
            pltpu.VMEM((tiles, 192, columns), F32),
            pltpu.VMEM(face, BF16),
            pltpu.VMEM(face, BF16),
            pltpu.VMEM(face, BF16),
            pltpu.VMEM((STEPS, tiles, 3, 16, columns), BF16),
            pltpu.VMEM((STEPS, 2, span_x, span_z, 48, columns), BF16),
            pltpu.VMEM((width, columns), F32),
            pltpu.VMEM((width, columns), BF16),
            pltpu.VMEM(block, BF16),
            pltpu.VMEM(block, BF16),
            pltpu.VMEM((STEPS,) + block, BF16),
            pltpu.VMEM((STEPS,) + block, BF16),
            pltpu.VMEM((STEPS,) + block, BF16),
            pltpu.VMEM((STEPS,) + block, BF16),
            pltpu.VMEM((n * 8, 128), F32),
            pltpu.VMEM((slots, 128), BF16),
            pltpu.VMEM((32, slots), BF16),
            dma((7,)),
            dma,
            dma((STEPS, span_y, 2)),
            dma((STEPS, span_y, 2)),
            dma((STEPS, 2)),
            dma((STEPS, 2)),
            dma,
            dma,
            dma((STEPS,)),
            dma((STEPS,)),
            dma((STEPS,)),
            dma((STEPS,)),
        ],
        compiler_params=pltpu.CompilerParams(
            collective_id=0, has_side_effects=True, vmem_limit_bytes=56 * 1024 * 1024
        ),
    )(
        adj,
        coup,
        inv,
        tile_mask,
        perf_cell,
        perf_slot,
        perf_live,
        perf_coef,
        well_gain,
        misfit,
    )
    out, rounded = pl.pallas_call(
        last_product,
        out_shape=(
            jax.ShapeDtypeStruct((tiles, 192, columns), BF16),
            jax.ShapeDtypeStruct(wells.shape, BF16),
        ),
        in_specs=[any_space] * 3,
        out_specs=(any_space, vmem),
        scratch_shapes=[
            pltpu.VMEM((tiles, 192, columns), BF16),
            pltpu.VMEM((tiles, 192, 192), BF16),
            pltpu.VMEM(wells.shape, F32),
            pltpu.VMEM((tiles, 192, columns), BF16),
            dma((tiles // 2, 2)),
            dma,
            dma,
        ],
        compiler_params=pltpu.CompilerParams(vmem_limit_bytes=56 * 1024 * 1024),
    )(source, inv, wells)
    return out.reshape(later_adjoint.shape), rounded


def solution(mesh):
    return jax.shard_map(
        functools.partial(local, mesh.shape["gx"], mesh.shape["gy"]),
        mesh=mesh,
        in_specs=(
            P("gx", "gy", None, None, None),
            P("gx", "gy", None, None, None, None),
            P("gx", "gy", None, None, None),
            P("gx", "gy", None, None),
            P(("gx", "gy"), None),
            P(("gx", "gy"), None),
            P(("gx", "gy"), None),
            P(None, ("gx", "gy"), None),
            P(("gx", "gy")),
            P(None, ("gx", "gy"), None),
        ),
        out_specs=(P("gx", "gy", None, None, None), P(None, ("gx", "gy"), None)),
        check_vma=False,
    )
```

```python
import functools
import jax
import jax.numpy as jnp
from jax import lax
from jax.experimental import pallas as pl
from jax.experimental.pallas import tpu as pltpu
from jax.sharding import PartitionSpec as P

CAPACITY = 2
STEPS = 2
MESH = pl.DeviceIdType.MESH
BF16 = jnp.bfloat16
F32 = jnp.float32
I32 = jnp.int32


def dot(a, b):
    return jnp.dot(a, b, preferred_element_type=F32)


def iota(shape, dim):
    return lax.broadcasted_iota(I32, shape, dim)


def kernel(
    n_gx,
    n_gy,
    adj_hbm,
    coup_hbm,
    inv_hbm,
    mask_ref,
    cell_ref,
    slot_ref,
    live_ref,
    coef_ref,
    gain_ref,
    misfit_hbm,
    source_hbm,
    wells_ref,
    adj0,
    adj1,
    outbuf,
    coup,
    inv,
    misfit,
    sel_face,
    gather_w,
    near_w,
    far_w,
    flux,
    face_ylo,
    face_yhi,
    face_z,
    halo_x,
    halo_y,
    message_acc,
    landed_rows,
    tag_out,
    tag_in,
    message_out,
    message_in,
    return_out,
    return_in,
    stage,
    sel_rows,
    sel_wells,
    load_sems,
    out_sem,
    x_send,
    x_recv,
    y_send,
    y_recv,
    tag_send,
    tag_recv,
    message_send,
    message_recv,
    return_send,
    return_recv,
):
    n = n_gx * n_gy
    slots = CAPACITY * n
    tiles = adj0.shape[0]
    span_y = face_z.shape[2]
    columns = adj0.shape[-1]
    lanes = 128
    chunks = columns // lanes
    piece = 256
    cuts = [slice(c, c + piece) for c in range(0, columns, piece)]
    gx = lax.axis_index("gx")
    gy = lax.axis_index("gy")
    me = gx * n_gy + gy

    quarter = tiles // 4
    loads = [
        pltpu.make_async_copy(
            adj_hbm.at[pl.ds(q * quarter, quarter)],
            adj0.at[pl.ds(q * quarter, quarter)],
            load_sems.at[q],
        )
        for q in range(4)
    ]
    load_coup = pltpu.make_async_copy(coup_hbm, coup, load_sems.at[4])
    load_inv = pltpu.make_async_copy(inv_hbm, inv, load_sems.at[5])
    load_misfit = pltpu.make_async_copy(misfit_hbm, misfit.at[:, pl.ds(0, 24)], load_sems.at[6])
    for load in loads + [load_coup, load_inv, load_misfit]:
        load.start()

    barrier = pltpu.get_barrier_semaphore()

    def greet(d, carry):
        j = lax.rem(me + d, n)
        pl.semaphore_signal(
            barrier, inc=1, device_id=(j // n_gy, lax.rem(j, n_gy)), device_id_type=MESH
        )
        return carry

    lax.fori_loop(1, n, greet, 0)

    def fill_tag(p, carry):
        upper = iota((8, lanes), 0) < 4
        tag_out[p] = jnp.where(upper, slot_ref[0, 2 * p], slot_ref[0, 2 * p + 1]).astype(F32).astype(BF16)
        return carry

    lax.fori_loop(0, n, fill_tag, 0)

    row = iota((48, 192), 0)
    col = iota((48, 192), 1)
    start_y = (row // 4) * 16 + row % 4
    pick_ylo = jnp.where(col == start_y, 1.0, 0.0).astype(BF16)
    pick_yhi = jnp.where(col == start_y + 12, 1.0, 0.0).astype(BF16)
    for z in range(2):
        sel_face[z, 0:48] = pick_ylo
        sel_face[z, 48:96] = pick_yhi
        sel_face[z, 96:144] = jnp.where(col == 4 * row + 3 * (1 - z), 1.0, 0.0).astype(BF16)

    cell_row = jnp.concatenate([cell_ref[...], cell_ref[...]], axis=1)
    parts = []
    for k in range(3):
        coef = coef_ref[k] * live_ref[...].astype(F32)
        high = coef.astype(BF16).astype(F32)
        low = (coef - high).astype(BF16).astype(F32)
        parts.append(jnp.concatenate([high, low], axis=1))
    width = 2 * slots
    cell_col = jnp.broadcast_to(cell_row, (lanes, width)).T
    cell_col = jnp.concatenate([cell_col, cell_col[:, 0:64]], axis=1)
    lane = iota((width, 192), 1)
    wide = [jnp.broadcast_to(part, (lanes, width)).T for part in parts]
    wide = [jnp.concatenate([w, w[:, 0:64]], axis=1) for w in wide]
    coef_cols = jnp.where(lane < 64, wide[0], jnp.where(lane < 128, wide[1], wide[2]))
    shifted_col = cell_col - lane % 64
    coef_rows = jnp.concatenate(
        [jnp.broadcast_to(part, (64, width)) for part in parts], axis=0
    )
    shifted_row = jnp.broadcast_to(cell_row, (192, width)) - iota((192, width), 0) % 64

    def place(t, carry):
        gather_w[t] = jnp.where(shifted_col == 64 * t, coef_cols, 0.0).astype(BF16)
        far_w[t, :, 0:width] = jnp.where(shifted_row == 64 * t, coef_rows, 0.0).astype(BF16)
        return carry

    lax.fori_loop(0, tiles, place, 0)
    misfit[:, 24:32] = jnp.zeros((STEPS, 8, columns), F32)

    half = tiles // 2

    @pl.when(gx == 0)
    def _():
        halo_x[:, 0:half] = jnp.zeros((STEPS, half) + halo_x.shape[2:], BF16)

    @pl.when(gx == n_gx - 1)
    def _():
        halo_x[:, half:tiles] = jnp.zeros((STEPS, half) + halo_x.shape[2:], BF16)

    @pl.when(gy == 0)
    def _():
        halo_y[:, 0] = jnp.zeros((STEPS,) + halo_y.shape[2:], BF16)

    @pl.when(gy == n_gy - 1)
    def _():
        halo_y[:, 1] = jnp.zeros((STEPS,) + halo_y.shape[2:], BF16)

    pl.semaphore_wait(barrier, n - 1)

    def spread(source, target, send, recv):
        own = pltpu.make_async_copy(source.at[me], target.at[me], recv)
        own.start()

        def one(d, carry):
            j = lax.rem(me + d, n)
            pltpu.make_async_remote_copy(
                src_ref=source.at[j],
                dst_ref=target.at[me],
                send_sem=send,
                recv_sem=recv,
                device_id=(j // n_gy, lax.rem(j, n_gy)),
                device_id_type=MESH,
            ).start()
            return carry

        lax.fori_loop(1, n, one, 0)

    def wait_all(target, recv):
        pltpu.make_async_copy(target, target, recv).wait()

    def wait_sent(source, send):
        part = source.at[pl.ds(0, n - 1)]
        pltpu.make_async_copy(part, part, send).wait()

    spread(tag_out, tag_in, tag_send, tag_recv)

    def x_copies(src, s, y):
        up = pltpu.make_async_remote_copy(
            src_ref=src.at[pl.ds(half + 2 * y, 2), :, 3],
            dst_ref=halo_x.at[s, pl.ds(2 * y, 2)],
            send_sem=x_send.at[s, y, 0],
            recv_sem=x_recv.at[s, y, 0],
            device_id=(gx + 1, gy),
            device_id_type=MESH,
        )
        down = pltpu.make_async_remote_copy(
            src_ref=src.at[pl.ds(2 * y, 2), :, 0],
            dst_ref=halo_x.at[s, pl.ds(half + 2 * y, 2)],
            send_sem=x_send.at[s, y, 1],
            recv_sem=x_recv.at[s, y, 1],
            device_id=(gx - 1, gy),
            device_id_type=MESH,
        )
        return up, down

    def y_copies(s):
        up = pltpu.make_async_remote_copy(
            src_ref=face_yhi.at[s, :, span_y - 1],
            dst_ref=halo_y.at[s, 0],
            send_sem=y_send.at[s, 0],
            recv_sem=y_recv.at[s, 0],
            device_id=(gx, gy + 1),
            device_id_type=MESH,
        )
        down = pltpu.make_async_remote_copy(
            src_ref=face_ylo.at[s, :, 0],
            dst_ref=halo_y.at[s, 1],
            send_sem=y_send.at[s, 1],
            recv_sem=y_recv.at[s, 1],
            device_id=(gx, gy - 1),
            device_id_type=MESH,
        )
        return up, down

    def for_pairs(y, body):
        for x in range(2):
            for z in range(2):
                body(x, z, (x * span_y + y) * 2 + z)

    y_order = [0, span_y - 1] + list(range(1, span_y - 1))

    def start_x(src, s, y):
        x_up, x_down = x_copies(src, s, y)

        @pl.when(gx < n_gx - 1)
        def _():
            x_up.start()

        @pl.when(gx > 0)
        def _():
            x_down.start()

    def faces(src, s, y):
        y_up, y_down = y_copies(s)

        def body(x, z, t):
            for cut in cuts:
                whole = src[t, :, :, :, cut].reshape(192, piece)
                got = dot(sel_face[z], whole)
                face_ylo[s, x, y, z, :, cut] = got[0:48].astype(BF16)
                face_yhi[s, x, y, z, :, cut] = got[48:96].astype(BF16)
                face_z[s, x, y, z, :, cut] = got[96:144].astype(BF16)
                term = dot(gather_w[t], whole)
                if y == 0 and x == 0 and z == 0:
                    message_acc[:, cut] = term
                else:
                    message_acc[:, cut] += term

        for_pairs(y, body)
        if y == 0:

            @pl.when(gy > 0)
            def _():
                y_down.start()

        if y == span_y - 1:

            @pl.when(gy < n_gy - 1)
            def _():
                y_up.start()

    for load in loads:
        load.wait()
    for y in y_order:
        start_x(adj0, 0, y)
        faces(adj0, 0, y)

    for s in range(STEPS):
        src = adj0 if s == 0 else adj1
        y_up, y_down = y_copies(s)

        message = message_acc[0:slots] + message_acc[slots:width]
        message = message.astype(BF16).astype(F32)
        for q in range(chunks):
            stage[pl.ds(q, slots, stride=chunks), :] = message[:, q * lanes : (q + 1) * lanes]
        message_out[s] = stage[...].reshape(n, 8, lanes).astype(BF16)
        spread(message_out.at[s], message_in.at[s], message_send.at[s], message_recv.at[s])

        if s == 0:
            load_coup.wait()

            def weights(y):
                def body(x, z, t):
                    def block(d):
                        keep = mask_ref[x, y, z, d] != 0
                        return jnp.where(keep, coup[t, d], jnp.zeros((48, 192), BF16))

                    near = [block(1 - x), block(5 - z)]
                    far = [block(x)]
                    (near if y > 0 else far).append(block(2))
                    (near if y < span_y - 1 else far).append(block(3))
                    near_w[t, :, 0 : 48 * len(near)] = jnp.concatenate(near, axis=0).T
                    far_w[t, :, width : width + 48 * len(far)] = jnp.concatenate(far, axis=0).T

                for_pairs(y, body)

        def near_flux(y):
            if s == 0:
                weights(y)

            def body(x, z, t):
                beside = ((1 - x) * span_y + y) * 2 + z
                for cut in cuts:
                    listed = [src[beside, :, 3 * x, :, cut].reshape(48, piece)]
                    listed.append(face_z[s, x, y, 1 - z, :, cut])
                    if y > 0:
                        listed.append(face_yhi[s, x, y - 1, z, :, cut])
                    if y < span_y - 1:
                        listed.append(face_ylo[s, x, y + 1, z, :, cut])
                    depth = 48 * len(listed)
                    flux[t, :, cut] = dot(near_w[t, :, 0:depth], jnp.concatenate(listed, axis=0))

            for_pairs(y, body)

        for y in y_order[:2]:
            near_flux(y)

        if s == 0:
            load_misfit.wait()
            wait_all(tag_in, tag_recv)
            stage[...] = tag_in[...].astype(F32).reshape(n * 8, lanes)
            tags = stage[pl.ds(0, slots, stride=4), :]
            chosen = jnp.where(tags.astype(I32) == iota((slots, lanes), 1), 1.0, 0.0)
            sel_rows[...] = chosen.astype(BF16)
            sel_wells[...] = chosen.T[0:32].astype(BF16)
        wait_all(message_in.at[s], message_recv.at[s])
        stage[...] = message_in[s].astype(F32).reshape(n * 8, lanes)
        arrived = jnp.concatenate(
            [stage[pl.ds(q, slots, stride=chunks), :] for q in range(chunks)], axis=1
        ).astype(BF16)
        gain_row = iota((32, 1), 0)
        gain = jnp.zeros((32, 1), F32)
        for w in range(24):
            gain = jnp.where(gain_row == w, gain_ref[w], gain)
        well = (gain * (dot(sel_wells[...], arrived) + misfit[s])).astype(BF16)
        wells_ref[s] = well.astype(F32)[0:24]
        returned = dot(sel_rows[:, 0:32], well)
        for q in range(chunks):
            stage[pl.ds(q, slots, stride=chunks), :] = returned[:, q * lanes : (q + 1) * lanes]
        return_out[s] = stage[...].reshape(n, 8, lanes).astype(BF16)
        spread(return_out.at[s], return_in.at[s], return_send.at[s], return_recv.at[s])
        for y in y_order[2:]:
            near_flux(y)

        if s == 0:
            load_inv.wait()
        wait_all(return_in.at[s], return_recv.at[s])
        stage[...] = return_in[s].astype(F32).reshape(n * 8, lanes)
        landed = jnp.concatenate(
            [stage[pl.ds(q, slots, stride=chunks), :] for q in range(chunks)], axis=1
        ).astype(BF16)
        landed_rows[0:slots] = landed
        landed_rows[slots:width] = landed

        def far_source(y, x, z, cut):
            t = (x * span_y + y) * 2 + z
            listed = [landed_rows[:, cut], halo_x[s, t, :, :, cut].reshape(48, piece)]
            if y == 0:
                listed.append(halo_y[s, 0, x, z, :, cut])
            if y == span_y - 1:
                listed.append(halo_y[s, 1, x, z, :, cut])
            depth = width + 48 * (len(listed) - 1)
            added = dot(far_w[t, :, 0:depth], jnp.concatenate(listed, axis=0))
            return (flux[t, :, cut] + added).astype(BF16)

        for y in y_order:
            x_up, x_down = x_copies(src, s, y)

            @pl.when(gx > 0)
            def _():
                x_up.wait_recv()

            @pl.when(gx < n_gx - 1)
            def _():
                x_down.wait_recv()

            if y == 0:

                @pl.when(gy > 0)
                def _():
                    y_up.wait_recv()

            if y == span_y - 1:

                @pl.when(gy < n_gy - 1)
                def _():
                    y_down.wait_recv()

            items = [(x, z, cut) for x in range(2) for z in range(2) for cut in cuts]
            ready = far_source(y, *items[0])
            for i, (x, z, cut) in enumerate(items):
                t = (x * span_y + y) * 2 + z
                source = ready
                if i + 1 < len(items):
                    ready = far_source(y, *items[i + 1])
                if s < STEPS - 1:
                    new = (-dot(inv[t], source)).astype(BF16)
                    adj1[t, :, :, :, cut] = new.reshape(3, 4, 16, piece)
                else:
                    outbuf[t, :, cut] = source
            if s < STEPS - 1:
                start_x(adj1, s + 1, y)
                faces(adj1, s + 1, y)
            else:
                for x in range(2):
                    rows = pl.ds((x * span_y + y) * 2, 2)
                    pltpu.make_async_copy(outbuf.at[rows], source_hbm.at[rows], out_sem).start()

    for s in range(STEPS):
        y_up, y_down = y_copies(s)
        for y in range(span_y):
            x_up, x_down = x_copies(adj0 if s == 0 else adj1, s, y)

            @pl.when(gx < n_gx - 1)
            def _():
                x_up.wait_send()

            @pl.when(gx > 0)
            def _():
                x_down.wait_send()

        @pl.when(gy < n_gy - 1)
        def _():
            y_up.wait_send()

        @pl.when(gy > 0)
        def _():
            y_down.wait_send()

        wait_sent(message_out.at[s], message_send.at[s])
        wait_sent(return_out.at[s], return_send.at[s])
    wait_sent(tag_out, tag_send)
    pltpu.make_async_copy(outbuf, source_hbm, out_sem).wait()


def last_product(
    source_hbm, inv_hbm, wells_hbm, out_hbm, rounded_ref, source, inv, wells, out, in_sems, wells_sem, out_sem
):
    tiles = source.shape[0]
    group = 2
    loads = []
    for g in range(tiles // group):
        rows = pl.ds(g * group, group)
        pair = (
            pltpu.make_async_copy(inv_hbm.at[rows], inv.at[rows], in_sems.at[g, 0]),
            pltpu.make_async_copy(source_hbm.at[rows], source.at[rows], in_sems.at[g, 1]),
        )
        for load in pair:
            load.start()
        loads.append(pair)
    load_wells = pltpu.make_async_copy(wells_hbm, wells, wells_sem)
    load_wells.start()
    for g, pair in enumerate(loads):
        for load in pair:
            load.wait()
        for t in range(g * group, (g + 1) * group):
            for c in range(0, source.shape[2], 256):
                cut = slice(c, c + 256)
                out[t, :, cut] = (-dot(inv[t], source[t, :, cut])).astype(BF16)
        rows = pl.ds(g * group, group)
        pltpu.make_async_copy(out.at[rows], out_hbm.at[rows], out_sem).start()
    load_wells.wait()
    rounded_ref[...] = wells[...].astype(BF16)
    pltpu.make_async_copy(out, out_hbm, out_sem).wait()


def local(
    n_gx,
    n_gy,
    later_adjoint,
    coupling,
    inverse_diag,
    tile_mask,
    perf_cell,
    perf_slot,
    perf_live,
    perf_coef,
    well_gain,
    misfit,
):
    span_x, span_y, span_z, unknowns, columns = later_adjoint.shape
    tiles = span_x * span_y * span_z
    n = n_gx * n_gy
    slots = CAPACITY * n
    width = 2 * slots
    adj = later_adjoint.reshape(tiles, 3, 4, 16, columns)
    coup = jnp.swapaxes(coupling.reshape(tiles, 6, 192, 48), 2, 3)
    inv = inverse_diag.reshape(tiles, 192, 192)
    any_space = pl.BlockSpec(memory_space=pl.ANY)
    vmem = pl.BlockSpec(memory_space=pltpu.VMEM)
    smem = pl.BlockSpec(memory_space=pltpu.SMEM)
    dma = pltpu.SemaphoreType.DMA
    block = (n, 8, 128)
    face = (STEPS, span_x, span_y, span_z, 48, columns)
    source, wells = pl.pallas_call(
        functools.partial(kernel, n_gx, n_gy),
        out_shape=(
            jax.ShapeDtypeStruct((tiles, 192, columns), BF16),
            jax.ShapeDtypeStruct((STEPS, 24, columns), F32),
        ),
        in_specs=[any_space] * 3 + [smem, vmem, smem, vmem, vmem, smem, any_space],
        out_specs=(any_space, vmem),
        scratch_shapes=[
            pltpu.VMEM(adj.shape, BF16),
            pltpu.VMEM(adj.shape, BF16),
            pltpu.VMEM((tiles, 192, columns), BF16),
            pltpu.VMEM(coup.shape, BF16),
            pltpu.VMEM(inv.shape, BF16),
            pltpu.VMEM((STEPS, 32, columns), F32),
            pltpu.VMEM((2, 144, 192), BF16),
            pltpu.VMEM((tiles, width, 192), BF16),
            pltpu.VMEM((tiles, 192, 192), BF16),
            pltpu.VMEM((tiles, 192, width + 96), BF16),
            pltpu.VMEM((tiles, 192, columns), F32),
            pltpu.VMEM(face, BF16),
            pltpu.VMEM(face, BF16),
            pltpu.VMEM(face, BF16),
            pltpu.VMEM((STEPS, tiles, 3, 16, columns), BF16),
            pltpu.VMEM((STEPS, 2, span_x, span_z, 48, columns), BF16),
            pltpu.VMEM((width, columns), F32),
            pltpu.VMEM((width, columns), BF16),
            pltpu.VMEM(block, BF16),
            pltpu.VMEM(block, BF16),
            pltpu.VMEM((STEPS,) + block, BF16),
            pltpu.VMEM((STEPS,) + block, BF16),
            pltpu.VMEM((STEPS,) + block, BF16),
            pltpu.VMEM((STEPS,) + block, BF16),
            pltpu.VMEM((n * 8, 128), F32),
            pltpu.VMEM((slots, 128), BF16),
            pltpu.VMEM((32, slots), BF16),
            dma((7,)),
            dma,
            dma((STEPS, span_y, 2)),
            dma((STEPS, span_y, 2)),
            dma((STEPS, 2)),
            dma((STEPS, 2)),
            dma,
            dma,
            dma((STEPS,)),
            dma((STEPS,)),
            dma((STEPS,)),
            dma((STEPS,)),
        ],
        compiler_params=pltpu.CompilerParams(
            collective_id=0, has_side_effects=True, vmem_limit_bytes=56 * 1024 * 1024
        ),
    )(
        adj,
        coup,
        inv,
        tile_mask,
        perf_cell,
        perf_slot,
        perf_live,
        perf_coef,
        well_gain,
        misfit,
    )
    out, rounded = pl.pallas_call(
        last_product,
        out_shape=(
            jax.ShapeDtypeStruct((tiles, 192, columns), BF16),
            jax.ShapeDtypeStruct(wells.shape, BF16),
        ),
        in_specs=[any_space] * 3,
        out_specs=(any_space, vmem),
        scratch_shapes=[
            pltpu.VMEM((tiles, 192, columns), BF16),
            pltpu.VMEM((tiles, 192, 192), BF16),
            pltpu.VMEM(wells.shape, F32),
            pltpu.VMEM((tiles, 192, columns), BF16),
            dma((tiles // 2, 2)),
            dma,
            dma,
        ],
        compiler_params=pltpu.CompilerParams(vmem_limit_bytes=56 * 1024 * 1024),
    )(source, inv, wells)
    return out.reshape(later_adjoint.shape), rounded


def solution(mesh):
    return jax.shard_map(
        functools.partial(local, mesh.shape["gx"], mesh.shape["gy"]),
        mesh=mesh,
        in_specs=(
            P("gx", "gy", None, None, None),
            P("gx", "gy", None, None, None, None),
            P("gx", "gy", None, None, None),
            P("gx", "gy", None, None),
            P(("gx", "gy"), None),
            P(("gx", "gy"), None),
            P(("gx", "gy"), None),
            P(None, ("gx", "gy"), None),
            P(("gx", "gy")),
            P(None, ("gx", "gy"), None),
        ),
        out_specs=(P("gx", "gy", None, None, None), P(None, ("gx", "gy"), None)),
        check_vma=False,
    )
```
